256 devices in a mesh: tile: 32 (over x, z_hi, core), chan: 8 (over y, z_lo).
Axes of the slice: x: 4, y: 4, z: 8 (z_hi: 4, z_lo: 2; z = z_hi * 2 + z_lo), core: 2. Of those that a mesh axis runs over, the one named last changes fastest.
Arguments:
- field: bfloat16 [128, 32, 32, 128], P(None, 'tile', 'chan'), may hold values from -6 to 6
- hidden_fine: bfloat16 [128, 32, 32, 128], P(None, 'tile', 'chan'), may hold values from -3 to 3
- seam_tile: int32 [32, 4], replicated, may hold values from -1 to 31, as said below
- seam_code: int32 [32, 4], replicated, may hold values from 0 to 7, as said below
- corner_tile: int32 [32, 4], replicated, may hold values from -1 to 31, as said below
- corner_cell: int32 [32, 4], replicated, may hold values from 0 to 255, as said below
- pair_list: int32 [32], replicated, may hold values from 0 to 31, as said below
- enc_weight: bfloat16 [9, 128, 128], replicated, may hold values from -0.1875 to 0.1875
- enc_bias: float32 [128], replicated, may hold values from -2 to 2
- gru_input: bfloat16 [9, 3, 128, 128], replicated, may hold values from -0.1875 to 0.1875
- gru_state: bfloat16 [9, 3, 128, 128], replicated, may hold values from -0.1875 to 0.1875
- gru_bias: float32 [2, 3, 128], replicated, may hold values from -3 to 3
- coarse_gain: float32 [128], replicated, may hold values from 0.1 to 1.9
- coarse_shift: float32 [128], replicated, may hold values from -3 to 3
- coarse_weight: bfloat16 [128, 128], replicated, may hold values from -0.5 to 0.5
- dec_weight: bfloat16 [9, 128, 256], replicated, may hold values from -0.125 to 0.125
- dec_bias: float32 [128], replicated, may hold values from -2 to 2
Outputs:
- field_next: bfloat16 [128, 32, 32, 128], P(None, 'tile', 'chan')
- hidden_next: bfloat16 [128, 32, 32, 128], P(None, 'tile', 'chan')
The draws below stay inside these ranges and needn't reach their ends.
Inputs may be any that keep to these rules, and one draw needn't show every extreme that they name: Tiles sit on a grid of 4 rows and 8 columns, closed along the columns, each stored either upright or turned by half a turn; seam_tile names the tile across each stored side, -1 across the grid's top and bottom rows. `seam_code`: the neighbour's side is top or bottom for a top or bottom side, left or right for a left or right side. `corner_tile`: -1 outside the grid's rows and at grid vertices where only three tiles meet. `corner_cell`: A corner cell of the named tile: 0, 127, 128 or 255; 0 where corner_tile is -1. `pair_list`: A tile in the same grid row; the pairing is mutual and no tile pairs with itself.
All inputs are finite; a program needn't handle non-finite values.
Results may differ from the reference program's by a relative error of at most 0.014.
Values may be sent and summed in bfloat16 or wider, within the bound.
A program may use at most 64 MiB of HBM per device.

```python
import jax
import jax.numpy as jnp
from jax import lax

C = 128
PY = 32
PX = 128
STEPS = 2
TILES = 32


def layout(key):
    columns = TILES // 4
    placing = jax.random.permutation(jax.random.fold_in(key, 101), TILES).astype(jnp.int32)
    located = jnp.argsort(placing).astype(jnp.int32)
    rotated = jax.random.randint(jax.random.fold_in(key, 102), (TILES,), 0, 2).astype(jnp.int32)
    return (placing, rotated, located // columns, located % columns, columns)


def seam_lists(key):
    placing, rotated, grid_row, grid_col, columns = layout(key)
    side_ids = jnp.arange(4, dtype=jnp.int32)[None, :]
    facing = side_ids ^ rotated[:, None]
    step_row = jnp.where(facing == 0, -1, jnp.where(facing == 1, 1, 0))
    step_col = jnp.where(facing == 2, -1, jnp.where(facing == 3, 1, 0))
    near_row = grid_row[:, None] + step_row
    near_col = (grid_col[:, None] + step_col) % columns
    validity = (near_row >= 0) & (near_row < 4)
    nearby = placing[jnp.clip(near_row, 0, 3) * columns + near_col]
    their_side = facing ^ 1 ^ rotated[nearby]
    flipped = rotated[:, None] ^ rotated[nearby]
    tiles_out = jnp.where(validity, nearby, -1).astype(jnp.int32)
    codes_out = jnp.where(validity, their_side * 2 + flipped, 0).astype(jnp.int32)
    return (tiles_out, codes_out)


def corner_lists(key):
    placing, rotated, grid_row, grid_col, columns = layout(key)
    corner_ids = jnp.arange(4, dtype=jnp.int32)[None, :]
    facing = corner_ids ^ 3 * rotated[:, None]
    lower = facing // 2
    righter = facing % 2
    near_row = grid_row[:, None] + 2 * lower - 1
    near_col = (grid_col[:, None] + 2 * righter - 1) % columns
    vertex_row = grid_row[:, None] + lower
    vertex_col = (grid_col[:, None] + righter) % columns
    meeting = (vertex_row % 2 == 0) & (vertex_col % 2 == 0)
    validity = (near_row >= 0) & (near_row < 4) & jnp.logical_not(meeting)
    nearby = placing[jnp.clip(near_row, 0, 3) * columns + near_col]
    theirs = facing ^ 3 ^ 3 * rotated[nearby]
    position = theirs // 2 * PX + theirs % 2 * (PX - 1)
    tiles_out = jnp.where(validity, nearby, -1).astype(jnp.int32)
    cells_out = jnp.where(validity, position, 0).astype(jnp.int32)
    return (tiles_out, cells_out)


def draw_seam_tile(key, part):
    return seam_lists(key)[0]


def draw_seam_code(key, part):
    return seam_lists(key)[1]


def draw_corner_tile(key, part):
    return corner_lists(key)[0]


def draw_corner_cell(key, part):
    return corner_lists(key)[1]


def draw_pair_list(key, part):
    placing, rotated, grid_row, grid_col, columns = layout(key)
    return placing[grid_row * columns + (grid_col ^ 1)].astype(jnp.int32)


def shard_levels(key, extent, shards, smallest, largest):
    def one(dim, parts):
        heights = jax.random.uniform(jax.random.fold_in(jax.random.fold_in(key, 6), dim), (parts,), jnp.float32, smallest / len(shards), largest / len(shards))
        return jnp.repeat(jnp.exp(heights), extent[dim] // parts).reshape((-1,) + (1,) * (len(extent) - dim - 1))

    factor_of = one(*shards[0])
    for cut in shards[1:]:
        factor_of = factor_of * one(*cut)
    return factor_of


def centred(key, extent, deviation, most, cuts=(), kind=jnp.bfloat16):
    array = deviation * jax.random.normal(key, extent, jnp.float32)
    if cuts:
        array = array * shard_levels(key, extent, cuts, -0.22, 0.18)
    return jnp.clip(array, -most, most).astype(kind)


def setup_inputs(seed: int = 0) -> dict:
    key_list = jax.random.split(jax.random.key(seed), 18)
    return {
        "field": centred(key_list[0], (C, TILES, PY, PX), 1.0, 6.0, ((1, 32), (2, 8))),
        "hidden_fine": centred(key_list[1], (C, TILES, PY, PX), 0.5, 3.0, ((1, 32), (2, 8))),
        "seam_tile": draw_seam_tile(jax.random.fold_in(key_list[17], 71), 0),
        "seam_code": draw_seam_code(jax.random.fold_in(key_list[17], 71), 0),
        "corner_tile": draw_corner_tile(jax.random.fold_in(key_list[17], 71), 0),
        "corner_cell": draw_corner_cell(jax.random.fold_in(key_list[17], 71), 0),
        "pair_list": draw_pair_list(jax.random.fold_in(key_list[17], 71), 0),
        "enc_weight": centred(key_list[7], (9, C, C), (9 * C) ** -0.5, 0.1875),
        "enc_bias": centred(key_list[8], (C,), 0.3, 2.0, (), jnp.float32),
        "gru_input": centred(key_list[9], (9, 3, C, C), (9 * C) ** -0.5, 0.1875),
        "gru_state": centred(key_list[10], (9, 3, C, C), (9 * C) ** -0.5, 0.1875),
        "gru_bias": centred(key_list[11], (2, 3, C), 0.5, 3.0, (), jnp.float32),
        "coarse_gain": jnp.clip(1.0 + 0.18 * jax.random.normal(key_list[12], (C,), jnp.float32), 0.1, 1.9),
        "coarse_shift": centred(key_list[13], (C,), 0.5, 3.0, (), jnp.float32),
        "coarse_weight": centred(key_list[14], (C, C), C ** -0.5, 0.5),
        "dec_weight": centred(key_list[15], (9, C, 2 * C), (18 * C) ** -0.5, 0.125),
        "dec_bias": centred(key_list[16], (C,), 0.3, 2.0, (), jnp.float32),
    }


def border(stacked, seam_tile, seam_code, corner_tile, corner_cell):
    depth = stacked.shape[0]
    height = stacked.shape[2]
    breadth = stacked.shape[3]
    rim_cells = jnp.concatenate([stacked[:, :, 0, :], stacked[:, :, height - 1, :], stacked[:, :, :, 0], stacked[:, :, :, breadth - 1]], axis=2)
    side_strips = []
    for side_id in range(4):
        length = breadth if side_id < 2 else height
        source_tile = seam_tile[:, side_id]
        source_rim = rim_cells[:, jnp.maximum(source_tile, 0), :]
        their_side = seam_code[:, side_id] // 2
        flipped = seam_code[:, side_id] % 2
        offset = jnp.where(their_side < 2, their_side * breadth, 2 * breadth + (their_side - 2) * height)
        stepping = jnp.arange(length, dtype=jnp.int32)
        gather_at = jnp.where(flipped[:, None] == 1, offset[:, None] + length - 1 - stepping[None, :], offset[:, None] + stepping[None, :]).astype(jnp.int32)
        gather_at = jnp.broadcast_to(gather_at[None], (depth,) + gather_at.shape)
        picked = jnp.take_along_axis(source_rim, gather_at, axis=2)
        side_strips.append(jnp.where((source_tile >= 0)[None, :, None], picked, jnp.zeros_like(picked)))
    corners = []
    for corner_id in range(4):
        source_tile = corner_tile[:, corner_id]
        source_rim = rim_cells[:, jnp.maximum(source_tile, 0), :]
        gather_at = jnp.broadcast_to(corner_cell[:, corner_id][None, :, None], (depth, source_tile.shape[0], 1)).astype(jnp.int32)
        picked = jnp.take_along_axis(source_rim, gather_at, axis=2)
        corners.append(jnp.where((source_tile >= 0)[None, :, None], picked, jnp.zeros_like(picked)))
    upper_row = jnp.concatenate([corners[0], side_strips[0], corners[1]], axis=2)
    lower_row = jnp.concatenate([corners[2], side_strips[1], corners[3]], axis=2)
    middle = jnp.concatenate([side_strips[2][..., None], stacked, side_strips[3][..., None]], axis=3)
    return jnp.concatenate([upper_row[:, :, None], middle, lower_row[:, :, None]], axis=2)

def convolve(padded, weight, spec_form):
    height = padded.shape[2] - 2
    breadth = padded.shape[3] - 2
    summed = None
    for tap_id in range(9):
        shift_row = tap_id // 3
        shift_col = tap_id % 3
        window = padded[:, :, shift_row:shift_row + height, shift_col:shift_col + breadth].astype(jnp.float32)
        tap_term = jnp.einsum(spec_form, weight[tap_id].astype(jnp.float32), window)
        summed = tap_term if summed is None else summed + tap_term
    return summed

def reference(field, hidden_fine, seam_tile, seam_code, corner_tile, corner_cell, pair_list, enc_weight, enc_bias, gru_input, gru_state, gru_bias, coarse_gain, coarse_shift, coarse_weight, dec_weight, dec_bias):
    channels = field.shape[0]
    state = field
    memory = hidden_fine
    for step_id in range(STEPS):
        padded = border(state, seam_tile, seam_code, corner_tile, corner_cell)
        encoded = jax.nn.gelu(convolve(padded, enc_weight, 'oi,ityx->otyx') + enc_bias[:, None, None, None]).astype(jnp.bfloat16)
        both_padded = border(jnp.concatenate([encoded, memory], axis=0), seam_tile, seam_code, corner_tile, corner_cell)
        from_input = convolve(both_padded[:channels], gru_input, 'goi,ityx->gotyx')
        from_state = convolve(both_padded[channels:], gru_state, 'goi,ityx->gotyx')
        biases = gru_bias[:, :, :, None, None, None]
        update = jax.nn.sigmoid(from_input[0] + biases[0, 0] + (from_state[0] + biases[1, 0]))
        reset = jax.nn.sigmoid(from_input[1] + biases[0, 1] + (from_state[1] + biases[1, 1]))
        candidate = jnp.tanh(from_input[2] + biases[0, 2] + reset * (from_state[2] + biases[1, 2]))
        memory = ((1.0 - update) * candidate + update * memory.astype(jnp.float32)).astype(jnp.bfloat16)
        coarse = memory.astype(jnp.float32).reshape(channels, TILES, PY // 2, 2, PX // 2, 2).sum(axis=(3, 5)) * 0.25
        sums_one = lax.optimization_barrier(jnp.sum(coarse, axis=(2, 3)))
        sums_two = lax.optimization_barrier(jnp.sum(coarse * coarse, axis=(2, 3)))
        counted = 2 * (PY // 2) * (PX // 2)
        average = (sums_one + sums_one[:, pair_list]) / counted
        spread = (sums_two + sums_two[:, pair_list]) / counted - average * average
        scaled = (coarse - average[:, :, None, None]) * lax.rsqrt(spread + 1e-05)[:, :, None, None] * coarse_gain[:, None, None, None] + coarse_shift[:, None, None, None]
        active = jax.nn.gelu(scaled).astype(jnp.bfloat16)
        mixed = jnp.einsum('oi,ityx->otyx', coarse_weight.astype(jnp.float32), active.astype(jnp.float32))
        lifted = (coarse + mixed).astype(jnp.bfloat16)
        upsampled = jnp.repeat(jnp.repeat(lifted, 2, axis=2), 2, axis=3)
        joined = border(jnp.concatenate([upsampled, memory], axis=0), seam_tile, seam_code, corner_tile, corner_cell)
        change = convolve(joined, dec_weight, 'oi,ityx->otyx') + dec_bias[:, None, None, None]
        state = (state.astype(jnp.float32) + change).astype(jnp.bfloat16)
    return (state, memory)
```

```python
import functools
import math

import jax
import jax.numpy as jnp
from jax import lax
from jax.experimental import pallas as pl
from jax.experimental.pallas import tpu as pltpu
from jax.sharding import PartitionSpec as P

STEPS = 2
LANES = 128
ROWS = 4
HALF = 64
F32 = jnp.float32
BF16 = jnp.bfloat16
MESH = pl.DeviceIdType.MESH


def gelu(x):
    inner = math.sqrt(2.0 / math.pi) * (x + 0.044715 * (x * x * x))
    return 0.5 * x * (1.0 + jnp.tanh(inner))


def sigmoid(x):
    return 0.5 + 0.5 * jnp.tanh(0.5 * x)


def flat(value):
    return value.reshape(-1, LANES)


def lane_ids(rows):
    return lax.broadcasted_iota(jnp.int32, (rows, LANES), 1)


def wait_for(ref, sem):
    pltpu.make_async_copy(ref, ref, sem).wait()


def three_parts(value):
    high = value.astype(BF16).astype(F32)
    rest = value - high
    middle = rest.astype(BF16).astype(F32)
    return high, middle, rest - middle


def split_tile(t, nz):
    return lax.div(t, 2 * nz), lax.rem(lax.div(t, 2), nz), lax.rem(t, 2)


class Place:
    def __init__(self, nx, nz, ranks):
        self.nx, self.nz, self.ranks = nx, nz, ranks
        self.t = lax.axis_index("tile")
        self.c = lax.axis_index("chan")
        self.x, self.z, self.k = split_tile(self.t, nz)
        self.i = self.x * 2 + self.k
        self.lines = 2 * nx

    def chan_peer(self, d):
        return lax.rem(self.c + d, self.ranks)

    def line_peer(self, d):
        other = lax.rem(self.i + d, self.lines)
        return lax.div(other, 2) * (2 * self.nz) + self.z * 2 + lax.rem(other, 2)

    def z_peer(self, d):
        other = lax.rem(self.z + d, self.nz)
        return self.x * (2 * self.nz) + other * 2 + self.k


class Round:
    def __init__(self, at, refs, arrays, extra, sel, turn, py):
        (self.cols_src, self.p1, self.r8, self.p3src, self.p3, self.h,
         self.up, self.dn, self.cols, self.upx, self.dnx, self.send, self.recv) = refs
        self.at, self.arrays, self.extra, self.sel, self.turn, self.py = at, arrays, extra, sel, turn, py
        self.a = len(arrays)

    def remote(self, src, dst, send, recv, t, c):
        return pltpu.make_async_remote_copy(
            src_ref=src, dst_ref=dst, send_sem=self.send.at[send], recv_sem=self.recv.at[recv],
            device_id=(t, c), device_id_type=MESH,
        )

    def local(self, src, dst, recv):
        return pltpu.make_async_copy(src, dst, self.recv.at[recv])

    def phase1(self, sums=None):
        at, py, ranks = self.at, self.py, self.at.ranks
        lanes = lane_ids(LANES)
        for a, (rows, deep) in enumerate(self.arrays):
            first, last = deep, rows.shape[0] - 1 - deep

            @pl.when(at.c < ranks - 1)
            def _():
                self.remote(rows.at[last], self.up.at[a], 3, 3, at.t, at.c + 1).start()

            @pl.when(at.c > 0)
            def _():
                self.remote(rows.at[first], self.dn.at[a], 4, 4, at.t, at.c - 1).start()

            @pl.when(at.c == 0)
            def _():
                self.local(rows.at[first, at.c], self.p1.at[ranks, a], 0).start()
                for d in range(1, ranks):
                    to = at.chan_peer(d)
                    self.remote(rows.at[first, to], self.p1.at[ranks, a], 1, 0, at.t, to).start()

            @pl.when(at.c == ranks - 1)
            def _():
                self.local(rows.at[last, at.c], self.p1.at[ranks + 1, a], 0).start()
                for d in range(1, ranks):
                    to = at.chan_peer(d)
                    self.remote(rows.at[last, to], self.p1.at[ranks + 1, a], 2, 0, at.t, to).start()

        for a, (rows, deep) in enumerate(self.arrays):
            each = ROWS // rows.shape[0]
            tile = jnp.zeros((LANES, LANES), F32)
            for q in range(ROWS):
                row = flat(rows[q // each]).astype(F32)
                tile = jnp.where(lanes == q, row[:, deep : deep + 1], tile)
                tile = jnp.where(lanes == LANES - py + q, row[:, LANES - 1 - deep : LANES - deep], tile)
            tile = pltpu.roll(tile, ROWS * at.c, 1)
            if sums is not None and a == self.a - 1:
                parts = three_parts(sums[0]) + three_parts(sums[1])
                for j, part in enumerate(parts):
                    tile = jnp.where(lanes == py + 6 * at.c + j, part, tile)
            self.cols_src[:, a] = tile.astype(BF16).reshape(ranks, -1, LANES)
        self.local(self.cols_src.at[at.c], self.p1.at[at.c], 0).start()
        for d in range(1, ranks):
            to = at.chan_peer(d)
            self.remote(self.cols_src.at[to], self.p1.at[at.c], 0, 0, at.t, to).start()

    def phase2(self, sums=False):
        at, py, ranks = self.at, self.py, self.at.ranks
        wait_for(self.p1, self.recv.at[0])
        self.r8[at.i, 0] = self.p1[ranks]
        self.r8[at.i, 1] = self.p1[ranks + 1]
        for a in range(self.a):
            merged = self.p1[0, a].astype(F32)
            for r in range(1, ranks):
                merged = merged + self.p1[r, a].astype(F32)
            if sums and a == self.a - 1:
                lanes = lane_ids(merged.shape[0])
                held = (lanes >= py) & (lanes < py + 6 * ranks)
                kind = lax.rem(lanes - py + 6 * LANES, 6) < 3
                total = jnp.sum(jnp.where(held & kind, merged, 0.0), axis=1, keepdims=True)
                square = jnp.sum(
                    jnp.where(held & jnp.logical_not(kind), merged, 0.0), axis=1, keepdims=True
                )
                merged = jnp.where(held, 0.0, merged)
                parts = three_parts(total) + three_parts(square)
                for j, part in enumerate(parts):
                    merged = jnp.where(lanes == py + 6 * at.i + j, part, merged)
            self.r8[at.i, 2, a] = merged.astype(BF16)
        for d in range(1, at.lines):
            self.remote(self.r8.at[at.i], self.r8.at[at.i], 5, 1, at.line_peer(d), at.c).start()

    def phase3(self, both, sums=False, deep=False):
        at, py = self.at, self.py
        width = py + 2
        wait_for(self.r8.at[pl.ds(0, at.lines - 1)], self.recv.at[1])
        count = 3 * at.lines
        held = self.r8[...].reshape((count,) + self.r8.shape[2:])
        both[pl.ds(0, count), pl.ds(0, self.a)] = held
        turned = jnp.dot(flat(held), self.turn[...], preferred_element_type=F32)
        both[pl.ds(count, count), pl.ds(0, self.a)] = turned.astype(BF16).reshape(held.shape)
        cut = self.r8.shape[3]
        lanes = lane_ids(self.a * cut).reshape(self.a, cut, LANES)

        def take(d, e):
            index = self.sel[d * 12 + e]
            value = both[jnp.maximum(index, 0), pl.ds(0, self.a)].astype(F32)
            return jnp.where(index >= 0, value, 0.0)

        def shift(value, by):
            return pltpu.roll(value, by % LANES, 2)

        base = jnp.zeros((self.a, cut, LANES), F32)
        if sums:
            gathered = self.r8[0, 2].astype(F32)
            for i in range(1, at.lines):
                gathered = gathered + self.r8[i, 2].astype(F32)
            gathered = shift(gathered, 2 * width - py)
            base = jnp.where((lanes >= 2 * width) & (lanes < 2 * width + 6 * at.lines), gathered, 0.0)

        def partial(d, dst):
            dst[0] = take(d, 0).astype(BF16)
            dst[1] = take(d, 1).astype(BF16)
            tile = base
            left = shift(take(d, 2), 1 + py)
            tile = jnp.where((lanes >= 1) & (lanes <= py), left, tile)
            right = shift(take(d, 3), width + 1)
            tile = jnp.where((lanes > width) & (lanes <= width + py), right, tile)
            for e, lane in ((4, 0), (5, width), (6, py + 1), (7, width + py + 1)):
                value = take(d, e + 4 if deep else e)
                tile = jnp.where(lanes == lane, shift(value, lane), tile)
                if deep:
                    beside = 2 * width + e - 4
                    tile = jnp.where(lanes == beside, shift(value, beside - 1), tile)
            dst[2] = tile.astype(BF16)

        for d in range(1, at.nz):
            partial(d, self.p3src.at[d - 1])
            self.remote(self.p3src.at[d - 1], self.p3.at[at.z], 6, 2, at.z_peer(d), at.c).start()
        partial(0, self.p3.at[at.z])

    def halo_sum(self):
        wait_for(self.p3.at[pl.ds(0, self.at.nz - 1)], self.recv.at[2])
        total = self.p3[0].astype(F32)
        for z in range(1, self.at.nz):
            total = total + self.p3[z].astype(F32)
        return total

    def phase4(self, total, extra=None):
        at, ranks = self.at, self.at.ranks
        for p in range(3):
            for a in range(self.a):
                self.h[p, a] = total[p, a].astype(BF16)
            if extra is not None:
                self.h[p, self.a] = extra[p].astype(BF16)
        self.local(self.h.at[2], self.cols.at[at.c], 5).start()
        for d in range(1, ranks):
            to = at.chan_peer(d)
            self.remote(self.h.at[2], self.cols.at[at.c], 7, 5, at.t, to).start()
        for side, rank, buf, bufx, sem in ((0, 0, self.up, self.upx, 3), (1, ranks - 1, self.dn, self.dnx, 4)):
            pieces = [(self.h.at[side, a], buf.at[a, at.c], 8 + side, sem) for a in range(self.a)]
            if self.extra:
                pieces.append((self.h.at[side, self.a], bufx.at[at.c], 8 + side, sem + 3))

            @pl.when(at.c == rank)
            def _():
                for src, dst, _, recv in pieces:
                    self.local(src, dst, recv).start()

            @pl.when(at.c != rank)
            def _():
                for src, dst, send, recv in pieces:
                    self.remote(src, dst, send, recv, at.t, rank).start()

    def finish(self):
        at = self.at
        wait_for(self.up, self.recv.at[3])
        wait_for(self.dn, self.recv.at[4])
        wait_for(self.cols, self.recv.at[5])
        if self.extra:

            @pl.when(at.c == 0)
            def _():
                wait_for(self.upx, self.recv.at[6])

            @pl.when(at.c == at.ranks - 1)
            def _():
                wait_for(self.dnx, self.recv.at[7])

    def slab_cols(self, a):
        value = flat(self.cols[:, a]).astype(F32)
        return pltpu.roll(value, lax.rem(LANES - ROWS * self.at.c, LANES), 1)

    def drain(self):
        at, ranks = self.at, self.at.ranks
        wait_for(self.p1.at[pl.ds(0, ranks - 1)], self.send.at[0])
        wait_for(self.r8.at[pl.ds(0, at.lines - 1)], self.send.at[5])
        wait_for(self.p3.at[pl.ds(0, at.nz - 1)], self.send.at[6])
        wait_for(self.cols.at[pl.ds(0, ranks - 1)], self.send.at[7])

        @pl.when(at.c == 0)
        def _():
            wait_for(self.p1.at[pl.ds(0, ranks - 1)], self.send.at[1])

        @pl.when(at.c == ranks - 1)
        def _():
            wait_for(self.p1.at[pl.ds(0, ranks - 1)], self.send.at[2])

        @pl.when(at.c < ranks - 1)
        def _():
            wait_for(self.up, self.send.at[3])
            wait_for(self.h.at[1], self.send.at[9])

        @pl.when(at.c > 0)
        def _():
            wait_for(self.dn, self.send.at[4])
            wait_for(self.h.at[0], self.send.at[8])


def round_scratch(a, a4, nx, nz, ranks, cut):
    vm = lambda *shape: pltpu.VMEM(shape + (cut, LANES), BF16)
    return [
        vm(ranks, a),
        vm(ranks + 2, a),
        vm(2 * nx, 3, a),
        vm(nz - 1, 3, a),
        vm(nz, 3, a),
        vm(3, a4),
        vm(a, ranks),
        vm(a, ranks),
        vm(ranks, a4),
        vm(ranks),
        vm(ranks),
        pltpu.SemaphoreType.DMA((10,)),
        pltpu.SemaphoreType.DMA((8,)),
    ]


ROUND_REFS = 13


def put_rows(stack, rows, cols, left_lane, right_lane, slots=None):
    lanes = lane_ids(LANES)
    for q, row in enumerate(rows):
        wide = row.astype(F32)
        here = pl.ds((q if slots is None else slots[q]) * LANES, LANES)
        first, last = left_lane + q, right_lane + q
        left = jnp.where(lanes == 0, cols[:, first : first + 1], pltpu.roll(wide, 1, 1))
        right = jnp.where(lanes == LANES - 1, cols[:, last : last + 1], pltpu.roll(wide, LANES - 1, 1))
        stack[pl.ds(0, LANES), here] = left.astype(BF16)
        stack[pl.ds(LANES, LANES), here] = row.astype(BF16)
        stack[pl.ds(2 * LANES, LANES), here] = right.astype(BF16)


def deep_cols(rnd, at, rows, py):
    width = py + 2
    lanes = lane_ids(LANES)
    near, far = flat(rnd.cols[:, 0]).astype(F32), flat(rnd.cols[:, 1]).astype(F32)

    def place(value):
        left = pltpu.roll(value, lax.rem(2 * LANES + 1 - ROWS * at.c, LANES), 1)
        right = pltpu.roll(value, lax.rem(2 * LANES + HALF + 1 - width - ROWS * at.c, LANES), 1)
        return jnp.where(lanes < HALF, left, right)

    one, two = place(near), place(far)
    top, bottom = at.c == 0, at.c == at.ranks - 1

    def put(tile, lane, value, source, where):
        return jnp.where(lanes == jnp.where(where, lane, -1), value[:, source : source + 1], tile)

    beside = 2 * width
    for base, corner, other in ((0, 0, py + 1), (HALF, width, width + py + 1)):
        n = 0 if base == 0 else 1
        one = put(one, base, far, corner, top)
        one = put(one, base + 7, far, other, bottom)
        two = put(two, base, far, beside + n, top)
        two = put(two, base + 1, near, beside + n, top)
        two = put(two, base + 6, near, beside + 2 + n, bottom)
        two = put(two, base + 7, far, beside + 2 + n, bottom)
    zero = jnp.zeros((LANES, LANES), F32)
    for q, row in enumerate(rows):
        wide = row.astype(F32)
        zero = jnp.where(lanes == q, wide[:, 0:1], zero)
        zero = jnp.where(lanes == HALF + q, wide[:, LANES - 1 :], zero)
    return zero, one, two


def edge_stack(edge, rows, cols, open_vertex):
    zero, one, two = cols
    lanes = lane_ids(LANES)
    hide = lambda tile, lane, n: jnp.where(lanes == jnp.where(open_vertex[n], lane, -1), 0.0, tile)
    upper = hide(hide(one, 2, 0), HALF + 2, 1)
    lower = hide(hide(one, 5, 2), HALF + 5, 3)
    put_rows(edge, rows[:3], upper, 0, HALF, (0, 3, 6))
    put_rows(edge, rows[5:], lower, 5, HALF + 5, (1, 4, 7))
    sides = (
        jnp.where(lanes < HALF, two, zero),
        one,
        jnp.where(lanes < HALF, zero, two),
    )
    for a in range(3):
        for b in range(3):
            tile = pltpu.roll(sides[b], LANES - a, 1) if a else sides[b]
            if a == 0 and b == 2:
                tile = hide(tile, 1, 0)
            if a == 0 and b == 0:
                tile = hide(tile, HALF + 1, 1)
            if a == 2 and b == 2:
                tile = hide(tile, 4, 2)
            if a == 2 and b == 0:
                tile = hide(tile, HALF + 4, 3)
            edge[pl.ds(b * LANES, LANES), pl.ds((3 * a + 2) * LANES, LANES)] = tile.astype(BF16)


def conv_rows(stack, weight, row, gates=None):
    summed = None
    for a in range(3):
        term = jnp.dot(
            weight(a), stack[:, pl.ds((row + a) * LANES, 2 * LANES)], preferred_element_type=F32
        )
        summed = term if summed is None else summed + term
    return summed


def kernel(dims, *refs):
    nx, nz, ranks, py = dims
    names = (
        "field", "hidden", "seam", "code", "corner", "cell", "pair", "enc_w", "gi_w", "gh_w", "dec_w",
        "mix_w", "enc_b", "gru_b", "gain", "shift", "dec_b", "turn", "state_out", "memory_out",
    )
    r = dict(zip(names, refs))
    scratch = list(refs[len(names) :])
    take = lambda n: [scratch.pop(0) for _ in range(n)]
    (we, wi, wh, wdl, wdm, s_state, s_mem, s_enc, s_lift, s_edge, gh, both, sel, wsem, vec) = take(15)
    mems, coarses, states = take(2), take(2), take(1)
    round_refs = [take(ROUND_REFS) for _ in range(4)]
    width = py + 2
    cut = LANES // ranks
    lanes = lane_ids(LANES)
    column = lambda j: vec[:, j : j + 1]

    at = Place(nx, nz, ranks)

    barrier = pltpu.get_barrier_semaphore()
    peers = [(at.t, at.chan_peer(d)) for d in range(1, ranks)]
    peers += [(at.line_peer(d), at.c) for d in range(1, at.lines)]
    peers += [(at.z_peer(d), at.c) for d in range(1, nz)]
    for peer in peers:
        pl.semaphore_signal(barrier, inc=1, device_id=peer, device_id_type=MESH)

    copies = []
    for tap in range(9):
        a, lane = tap // 3, pl.ds(tap % 3 * LANES, LANES)
        copies += [
            pltpu.make_async_copy(r["enc_w"].at[tap], we.at[a, pl.ds(0, LANES), lane], wsem.at[0]),
            pltpu.make_async_copy(r["enc_w"].at[8 - tap], we.at[a, pl.ds(LANES, LANES), lane], wsem.at[0]),
            pltpu.make_async_copy(r["gi_w"].at[tap], wi.at[a, :, :, lane], wsem.at[1]),
            pltpu.make_async_copy(r["gh_w"].at[tap], wh.at[a, :, :, lane], wsem.at[2]),
            pltpu.make_async_copy(r["dec_w"].at[tap, :, pl.ds(0, LANES)], wdl.at[a, :, lane], wsem.at[3]),
            pltpu.make_async_copy(
                r["dec_w"].at[tap, :, pl.ds(LANES, LANES)], wdm.at[a, :, lane], wsem.at[4]
            ),
        ]
    for copy in copies:
        copy.start()

    for d in range(nz):
        dest = at.z_peer(d)
        for side in range(4):
            source = r["seam"][side, dest]
            code = r["code"][side, dest]
            sx, sz, sk = split_tile(jnp.maximum(source, 0), nz)
            piece = lax.div(code, 2) if side < 2 else 2
            index = (lax.rem(code, 2) * at.lines + sx * 2 + sk) * 3 + piece
            sel[d * 12 + side] = jnp.where((source >= 0) & (sz == at.z), index, -1)
        for corner in range(4):
            source = r["corner"][corner, dest]
            cell = r["cell"][corner, dest]
            sx, sz, sk = split_tile(jnp.maximum(source, 0), nz)
            flip = jnp.where(lax.rem(cell, LANES) > 0, 1, 0)
            index = (flip * at.lines + sx * 2 + sk) * 3 + lax.div(cell, LANES)
            sel[d * 12 + 4 + corner] = jnp.where((source >= 0) & (sz == at.z), index, -1)
            row_side, col_side = corner // 2, 2 + corner % 2
            near = r["seam"][row_side, dest]
            turned = lax.rem(r["code"][row_side, dest], 2)
            near_held = jnp.maximum(near, 0)
            hop = lambda table: jnp.where(
                turned == 1, r[table][5 - col_side, near_held], r[table][col_side, near_held]
            )
            source = hop("seam")
            turned = lax.rem(turned + lax.rem(hop("code"), 2), 2)
            theirs = jnp.where(turned == 1, corner, 3 - corner)
            sx, sz, sk = split_tile(jnp.maximum(source, 0), nz)
            index = (lax.rem(theirs, 2) * at.lines + sx * 2 + sk) * 3 + lax.div(theirs, 2)
            sel[d * 12 + 8 + corner] = jnp.where((near >= 0) & (source >= 0) & (sz == at.z), index, -1)

    gru_b = r["gru_b"]
    listed = [
        r["enc_b"][...], gru_b[0, 0:1] + gru_b[0, 1:2], gru_b[1, 0:1] + gru_b[1, 1:2], gru_b[2, 0:1],
        gru_b[2, 1:2], r["gain"][...], r["shift"][...], r["dec_b"][...],
    ]
    vec[...] = jnp.transpose(jnp.concatenate(listed + [jnp.zeros((LANES - 8, LANES), F32)], axis=0))

    pl.semaphore_wait(barrier, len(peers))

    def make_round(n, arrays, extra=False):
        return Round(at, round_refs[n], arrays, extra, sel, r["turn"], py)

    def body_rows(rows, rnd, a):
        return [flat(rnd.up[a])] + [flat(rows[q]) for q in range(ROWS)] + [flat(rnd.dn[a])]

    def close_vertices(cols, left, right):
        for n, lane in enumerate((left, right, left + ROWS + 1, right + ROWS + 1)):
            cols = jnp.where(lanes == jnp.where(open_vertex[n], lane, -1), 0.0, cols)
        return cols

    def stack_rows(rows, rnd, a, stack, vertices=False):
        cols = rnd.slab_cols(a)
        if vertices:
            cols = close_vertices(cols, 0, width)
        put_rows(stack, body_rows(rows, rnd, a), cols, 0, width)

    first_rank, last_rank = at.c == 0, at.c == ranks - 1
    seams = [r["seam"][s, at.t] for s in range(4)]
    corners = [r["corner"][s, at.t] for s in range(4)]
    ranked = (first_rank, first_rank, last_rank, last_rank)
    odd = [lax.rem(r["code"][s, at.t], 2) == 1 for s in range(4)]
    turned_rows = (first_rank & odd[0], last_rank & odd[1])
    turned_cols = jnp.where(lanes < HALF, jnp.where(odd[2], 1, 0), jnp.where(odd[3], 1, 0))
    for n, (lane, cell) in enumerate(((0, 0), (HALF, LANES - 1), (ROWS + 1, LANES), (HALF + ROWS + 1, 2 * LANES - 1))):
        turned_here = jnp.where(r["cell"][n, at.t] == cell, 1, 0)
        turned_cols = jnp.where(lanes == jnp.where(ranked[n], lane, -1), turned_here, turned_cols)
    open_vertex = [rank & (corner < 0) for rank, corner in zip(ranked, corners)]

    def stack_state(rows, rnd):
        body = [flat(rnd.up[1])] + body_rows(rows, rnd, 0) + [flat(rnd.dn[1])]
        cols = deep_cols(rnd, at, body, py)
        put_rows(s_state, body[1:7], close_vertices(cols[1], 1, HALF + 1), 1, HALF + 1)
        edge_stack(s_edge, body, cols, open_vertex)

    def state_conv(gate):
        for n in range(2):
            gh[gate, :, pl.ds(2 * n * LANES, 2 * LANES)] = conv_rows(s_mem, lambda a: wh[a, gate], 2 * n)

    rounds = []
    rnd = make_round(0, [(r["field"], 0), (r["field"], 1), (r["hidden"], 0)])
    rounds.append(rnd)
    rnd.phase1()
    rnd.phase2()
    rnd.phase3(both, deep=True)
    rnd.phase4(rnd.halo_sum())
    rnd.finish()
    stack_state(r["field"], rnd)
    stack_rows(r["hidden"], rnd, 2, s_mem, True)
    wait_for(wh, wsem.at[2])
    for gate in range(3):
        state_conv(gate)
    wait_for(we, wsem.at[0])
    wait_for(wi, wsem.at[1])
    state, memory = r["field"], r["hidden"]

    for step in range(STEPS):
        encoded = []
        for n in range(2):
            acc = gelu(conv_rows(s_state, lambda a: we[a, :LANES], 2 * n) + column(0)).astype(BF16)
            encoded += [acc[:, :LANES], acc[:, LANES:]]
        edge = None
        for a in range(3):
            term = jnp.dot(we[a], s_edge[:, pl.ds(3 * a * LANES, 3 * LANES)], preferred_element_type=F32)
            edge = term if edge is None else edge + term
        bias = column(0)
        pick = lambda n, there: gelu(
            jnp.where(there, edge[LANES:, n * LANES : (n + 1) * LANES], edge[:LANES, n * LANES : (n + 1) * LANES])
            + bias
        )
        above, below, beside = pick(0, turned_rows[0]), pick(1, turned_rows[1]), pick(2, turned_cols > 0)
        above = jnp.where(first_rank & (seams[0] < 0), 0.0, above).astype(BF16)
        below = jnp.where(last_rank & (seams[1] < 0), 0.0, below).astype(BF16)
        beside = jnp.where(lanes < jnp.where(seams[2] < 0, HALF, 0), 0.0, beside)
        beside = jnp.where(lanes >= jnp.where(seams[3] < 0, HALF, LANES), 0.0, beside)
        beside = close_vertices(beside, 0, HALF)
        put_rows(s_enc, [above] + encoded + [below], beside, 0, HALF)

        fresh = mems[step]
        coarse_rows = []
        for n in range(2):
            here = pl.ds(2 * n * LANES, 2 * LANES)
            gate = [conv_rows(s_enc, lambda a: wi[a, g], 2 * n) for g in range(3)]
            update = sigmoid(gate[0] + gh[0, :, here] + column(1))
            reset = sigmoid(gate[1] + gh[1, :, here] + column(2))
            candidate = jnp.tanh(gate[2] + column(3) + reset * (gh[2, :, here] + column(4)))
            pair = None
            for q in range(2):
                cut_row = slice(q * LANES, (q + 1) * LANES)
                before = flat(memory[2 * n + q]).astype(F32)
                after = (1.0 - update[:, cut_row]) * candidate[:, cut_row] + update[:, cut_row] * before
                after = after.astype(BF16)
                fresh[2 * n + q] = after.reshape(fresh.shape[1:])
                after = after.astype(F32)
                pair = after if pair is None else pair + after
            other = jnp.where(lax.rem(lanes, 2) == 0, pltpu.roll(pair, LANES - 1, 1), pltpu.roll(pair, 1, 1))
            coarse_rows.append((pair + other) * 0.25)
        coarse = coarses[step]
        for n in range(2):
            coarse[n] = coarse_rows[n].astype(BF16).reshape(coarse.shape[1:])
        sums = (
            0.5 * jnp.sum(coarse_rows[0] + coarse_rows[1], axis=1, keepdims=True),
            0.5
            * jnp.sum(
                coarse_rows[0] * coarse_rows[0] + coarse_rows[1] * coarse_rows[1], axis=1, keepdims=True
            ),
        )

        rnd = make_round(1 + 2 * step, [(fresh, 0), (coarse, 0)], extra=True)
        rounds.append(rnd)
        rnd.phase1(sums)
        rnd.phase2(True)
        rnd.phase3(both, True)
        total = rnd.halo_sum()
        thin = lane_ids(cut)
        slice_here = pl.ds(pl.multiple_of(at.c * cut, cut), cut)
        gain, shift = vec[slice_here, 5:6], vec[slice_here, 6:7]

        def joint(tile):
            tile = jnp.maximum(tile, 0)
            picked = []
            for one in (tile, r["pair"][tile]):
                tx, tz, tk = split_tile(one, nz)
                lane = thin - (2 * width + 6 * (tx * 2 + tk))
                picked.append((rnd.p3[tz, 2, 1].astype(F32), lane))
            result = []
            for low in (0, 3):
                masked = sum(
                    jnp.where((lane >= low) & (lane < low + 3), value, 0.0) for value, lane in picked
                )
                result.append(jnp.sum(masked, axis=1, keepdims=True))
            counted = 2 * (py // 2) * (LANES // 2)
            average = result[0] / counted
            spread = result[1] / counted - average * average
            return average, lax.rsqrt(spread + 1e-05)

        own = joint(at.t)
        stats = [joint(tile) for tile in seams + corners]

        def norm(value, average, scale):
            return gelu((value - average) * scale * gain + shift)

        extra = []
        for side in range(2):
            value = norm(total[side, 1], *stats[side])
            extra.append(jnp.where(seams[side] >= 0, value, 0.0))
        average = jnp.zeros((cut, LANES), F32)
        scale = jnp.zeros((cut, LANES), F32)
        valid = jnp.zeros((cut, LANES), F32)
        spans = ((2, 1, py), (3, width + 1, py), (4, 0, 1), (5, width, 1), (6, py + 1, 1), (7, width + py + 1, 1))
        for e, begin, length in spans:
            inside = (thin >= begin) & (thin < begin + length)
            average = jnp.where(inside, stats[e][0], average)
            scale = jnp.where(inside, stats[e][1], scale)
            flag = jnp.where((seams + corners)[e] >= 0, 1.0, 0.0)
            valid = jnp.where(inside, flag, valid)
        extra.append(jnp.where(valid > 0.0, norm(total[2, 1], average, scale), 0.0))
        colour = total[2, 1]
        for j, part in enumerate(three_parts(own[0]) + three_parts(own[1])):
            colour = jnp.where(thin == 2 * width + j, part, colour)
        pieces = [[total[p, a] for a in range(2)] for p in range(3)]
        pieces[2][1] = colour
        rnd.phase4_pieces = pieces
        phase4_from(rnd, pieces, extra)
        rnd.finish()

        raw = flat(rnd.cols[:, 1]).astype(F32)
        stat_lane = lanes - 2 * width
        mean = jnp.sum(jnp.where((stat_lane >= 0) & (stat_lane < 3), raw, 0.0), axis=1, keepdims=True)
        inverse = jnp.sum(jnp.where((stat_lane >= 3) & (stat_lane < 6), raw, 0.0), axis=1, keepdims=True)
        wide = lambda value: gelu((value - mean) * inverse * column(5) + column(6))
        top, bottom = flat(rnd.up[1]).astype(F32), flat(rnd.dn[1]).astype(F32)
        active = [
            jnp.where(first_rank, flat(rnd.upx[...]).astype(F32), wide(top)),
            wide(coarse_rows[0]),
            wide(coarse_rows[1]),
            jnp.where(last_rank, flat(rnd.dnx[...]).astype(F32), wide(bottom)),
            rnd.slab_cols(2),
        ]
        base = [top, coarse_rows[0], coarse_rows[1], bottom, rnd.slab_cols(1)]
        lifted = [
            (b + jnp.dot(r["mix_w"][...], v.astype(BF16), preferred_element_type=F32)).astype(BF16)
            for b, v in zip(base, active)
        ]
        body = [lifted[0], lifted[1], lifted[1], lifted[2], lifted[2], lifted[3]]
        put_rows(s_lift, body, lifted[4].astype(F32), 0, width)
        stack_rows(fresh, rnd, 0, s_mem)

        if step == 0:
            wait_for(wdl, wsem.at[3])
            wait_for(wdm, wsem.at[4])
        result = r["state_out"] if step == STEPS - 1 else states[step]
        for n in range(2):
            acc = conv_rows(s_lift, lambda a: wdl[a], 2 * n) + conv_rows(s_mem, lambda a: wdm[a], 2 * n)
            acc = acc + column(7)
            for q in range(2):
                before = flat(state[2 * n + q]).astype(F32)
                after = (before + acc[:, q * LANES : (q + 1) * LANES]).astype(BF16)
                result[2 * n + q] = after.reshape(result.shape[1:])
        state, memory = result, fresh
        if step < STEPS - 1:
            rnd = make_round(2 + 2 * step, [(state, 0), (state, 1)])
            rounds.append(rnd)
            rnd.phase1()
            state_conv(0)
            rnd.phase2()
            state_conv(1)
            rnd.phase3(both, deep=True)
            state_conv(2)
            rnd.phase4(rnd.halo_sum())
            rnd.finish()
            stack_state(state, rnd)

    r["memory_out"][...] = memory[...]
    for rnd in rounds:
        rnd.drain()


def phase4_from(rnd, pieces, extra):
    rnd.phase4(Pieces(pieces), extra)


class Pieces:
    def __init__(self, pieces):
        self.pieces = pieces

    def __getitem__(self, key):
        return self.pieces[key[0]][key[1]]


def on_device(
    nx, nz, ranks, py,
    field, hidden_fine, seam_tile, seam_code, corner_tile, corner_cell, pair_list, enc_weight, enc_bias,
    gru_input, gru_state, gru_bias, coarse_gain, coarse_shift, coarse_weight, dec_weight, dec_bias,
):
    cut = LANES // ranks
    rows = lambda v: jnp.transpose(v[:, 0], (1, 0, 2)).reshape(ROWS, ranks, cut, LANES)
    turn = jnp.asarray(jnp.arange(LANES)[:, None] + jnp.arange(LANES)[None, :] == LANES - 1, BF16)
    vmem, smem, anywhere = (pl.BlockSpec(memory_space=s) for s in (pltpu.VMEM, pltpu.SMEM, pl.ANY))
    slab = (ROWS, ranks, cut, LANES)
    scratch = [
        pltpu.VMEM((3, 2 * LANES, 3 * LANES), BF16),
        pltpu.VMEM((3, 3, LANES, 3 * LANES), BF16),
        pltpu.VMEM((3, 3, LANES, 3 * LANES), BF16),
        pltpu.VMEM((3, LANES, 3 * LANES), BF16),
        pltpu.VMEM((3, LANES, 3 * LANES), BF16),
    ]
    scratch += [pltpu.VMEM((3 * LANES, 6 * LANES), BF16) for _ in range(4)]
    scratch += [pltpu.VMEM((3 * LANES, 9 * LANES), BF16)]
    scratch += [
        pltpu.VMEM((3, LANES, ROWS * LANES), F32),
        pltpu.VMEM((2 * 3 * 2 * nx, 3, cut, LANES), BF16),
        pltpu.SMEM((nz * 12,), jnp.int32),
        pltpu.SemaphoreType.DMA((5,)),
        pltpu.VMEM((LANES, LANES), F32),
    ]
    scratch += [pltpu.VMEM(slab, BF16) for _ in range(2)]
    scratch += [pltpu.VMEM((2, ranks, cut, LANES), BF16) for _ in range(2)]
    scratch += [pltpu.VMEM(slab, BF16)]
    for a, a4 in ((3, 3), (2, 3), (2, 2), (2, 3)):
        scratch += round_scratch(a, a4, nx, nz, ranks, cut)
    state, memory = pl.pallas_call(
        functools.partial(kernel, (nx, nz, ranks, py)),
        out_shape=[jax.ShapeDtypeStruct(slab, BF16)] * 2,
        in_specs=[vmem] * 2 + [smem] * 5 + [anywhere] * 4 + [vmem] * 7,
        out_specs=[vmem] * 2,
        scratch_shapes=scratch,
        compiler_params=pltpu.CompilerParams(
            collective_id=0, has_side_effects=True, vmem_limit_bytes=60 * 2**20
        ),
    )(
        rows(field), rows(hidden_fine), seam_tile.T, seam_code.T, corner_tile.T, corner_cell.T, pair_list,
        enc_weight, gru_input, gru_state, dec_weight, coarse_weight,
        enc_bias[None], jnp.transpose(gru_bias, (1, 0, 2)), coarse_gain[None], coarse_shift[None],
        dec_bias[None], turn,
    )
    back = lambda v: jnp.transpose(v.reshape(ROWS, LANES, LANES), (1, 0, 2))[:, None]
    return back(state), back(memory)


def solution(mesh):
    ranks = mesh.shape["chan"]
    tiles = mesh.shape["tile"]
    nz = 4 if tiles == 32 else 2
    nx = tiles // (2 * nz)
    placed = (P(None, "tile", "chan", None),) * 2
    return jax.shard_map(
        functools.partial(on_device, nx, nz, ranks, ROWS * ranks),
        mesh=mesh,
        in_specs=placed + (P(),) * 15,
        out_specs=placed,
        check_vma=False,
    )
```

```python
import functools
import math

import jax
import jax.numpy as jnp
from jax import lax
from jax.experimental import pallas as pl
from jax.experimental.pallas import tpu as pltpu
from jax.sharding import PartitionSpec as P

STEPS = 2
LANES = 128
ROWS = 4
HALF = 64
F32 = jnp.float32
BF16 = jnp.bfloat16
MESH = pl.DeviceIdType.MESH


def gelu(x):
    inner = math.sqrt(2.0 / math.pi) * (x + 0.044715 * (x * x * x))
    return 0.5 * x * (1.0 + jnp.tanh(inner))


def sigmoid(x):
    return 0.5 + 0.5 * jnp.tanh(0.5 * x)


def flat(value):
    return value.reshape(-1, LANES)


def lane_ids(rows):
    return lax.broadcasted_iota(jnp.int32, (rows, LANES), 1)


def wait_for(ref, sem):
    pltpu.make_async_copy(ref, ref, sem).wait()


def three_parts(value):
    high = value.astype(BF16).astype(F32)
    rest = value - high
    middle = rest.astype(BF16).astype(F32)
    return high, middle, rest - middle


def split_tile(t, nz):
    return lax.div(t, 2 * nz), lax.rem(lax.div(t, 2), nz), lax.rem(t, 2)


class Place:
    def __init__(self, nx, nz, ranks):
        self.nx, self.nz, self.ranks = nx, nz, ranks
        self.t = lax.axis_index("tile")
        self.c = lax.axis_index("chan")
        self.x, self.z, self.k = split_tile(self.t, nz)
        self.i = self.x * 2 + self.k
        self.lines = 2 * nx

    def chan_peer(self, d):
        return lax.rem(self.c + d, self.ranks)

    def line_peer(self, d):
        other = lax.rem(self.i + d, self.lines)
        return lax.div(other, 2) * (2 * self.nz) + self.z * 2 + lax.rem(other, 2)

    def z_peer(self, d):
        z, k = lax.rem(self.z + d // 2, self.nz), lax.rem(self.k + d % 2, 2)
        return self.x * (2 * self.nz) + z * 2 + k


class Round:
    def __init__(self, at, refs, arrays, extra, sel, turn, py):
        (self.cols_src, self.p1, self.own, self.r8, self.p3src, self.p3, self.h,
         self.up, self.dn, self.cols, self.upx, self.dnx, self.send, self.recv) = refs
        self.at, self.arrays, self.extra, self.sel, self.turn, self.py = at, arrays, extra, sel, turn, py
        self.a = len(arrays)

    def remote(self, src, dst, send, recv, t, c):
        return pltpu.make_async_remote_copy(
            src_ref=src, dst_ref=dst, send_sem=self.send.at[send], recv_sem=self.recv.at[recv],
            device_id=(t, c), device_id_type=MESH,
        )

    def local(self, src, dst, recv):
        return pltpu.make_async_copy(src, dst, self.recv.at[recv])

    def columns(self, sums=None):
        at, py, ranks = self.at, self.py, self.at.ranks
        lanes = lane_ids(LANES)
        for a, (rows, deep) in enumerate(self.arrays):
            each = ROWS // rows.shape[0]
            tile = jnp.zeros((LANES, LANES), F32)
            for q in range(ROWS):
                row = flat(rows[q // each]).astype(F32)
                tile = jnp.where(lanes == q, row[:, deep : deep + 1], tile)
                tile = jnp.where(lanes == LANES - py + q, row[:, LANES - 1 - deep : LANES - deep], tile)
            tile = pltpu.roll(tile, ROWS * at.c, 1)
            if sums is not None and a == self.a - 1:
                parts = three_parts(sums[0]) + three_parts(sums[1])
                for j, part in enumerate(parts):
                    tile = jnp.where(lanes == py + 6 * at.c + j, part, tile)
            self.cols_src[:, a] = tile.astype(BF16).reshape(ranks, -1, LANES)

    def phase1(self, columns=None):
        at, ranks = self.at, self.at.ranks
        for a, (rows, deep) in enumerate(self.arrays):
            first, last = deep, rows.shape[0] - 1 - deep

            @pl.when(at.c < ranks - 1)
            def _():
                self.remote(rows.at[last], self.up.at[a], 3, 3, at.t, at.c + 1).start()

            @pl.when(at.c > 0)
            def _():
                self.remote(rows.at[first], self.dn.at[a], 4, 4, at.t, at.c - 1).start()

            @pl.when(at.c == 0)
            def _():
                self.local(rows.at[first, at.c], self.p1.at[ranks, a], 0).start()
                for d in range(1, ranks):
                    to = at.chan_peer(d)
                    self.remote(rows.at[first, to], self.p1.at[ranks, a], 1, 0, at.t, to).start()

            @pl.when(at.c == ranks - 1)
            def _():
                self.local(rows.at[last, at.c], self.p1.at[ranks + 1, a], 0).start()
                for d in range(1, ranks):
                    to = at.chan_peer(d)
                    self.remote(rows.at[last, to], self.p1.at[ranks + 1, a], 2, 0, at.t, to).start()

        if columns is not None:
            columns()
        self.local(self.cols_src.at[at.c], self.p1.at[at.c], 0).start()
        for d in range(1, ranks):
            to = at.chan_peer(d)
            self.remote(self.cols_src.at[to], self.p1.at[at.c], 0, 0, at.t, to).start()

    def phase2(self, sums=False):
        at, py, ranks = self.at, self.py, self.at.ranks
        wait_for(self.p1, self.recv.at[0])
        for a in range(self.a):
            self.own[a, 0] = self.p1[ranks, a]
            self.own[a, 1] = self.p1[ranks + 1, a]
            merged = self.p1[0, a].astype(F32)
            for r in range(1, ranks):
                merged = merged + self.p1[r, a].astype(F32)
            if sums and a == self.a - 1:
                lanes = lane_ids(merged.shape[0])
                held = (lanes >= py) & (lanes < py + 6 * ranks)
                kind = lax.rem(lanes - py + 6 * LANES, 6) < 3
                total = jnp.sum(jnp.where(held & kind, merged, 0.0), axis=1, keepdims=True)
                square = jnp.sum(
                    jnp.where(held & jnp.logical_not(kind), merged, 0.0), axis=1, keepdims=True
                )
                merged = jnp.where(held, 0.0, merged)
                parts = three_parts(total) + three_parts(square)
                for j, part in enumerate(parts):
                    merged = jnp.where(lanes == py + 6 * at.i + j, part, merged)
            self.own[a, 2] = merged.astype(BF16)
        self.local(self.own.at[at.k], self.r8.at[at.i], 1).start()
        for d in range(1, at.lines):
            to = at.line_peer(d)
            self.remote(self.own.at[lax.rem(to, 2)], self.r8.at[at.i], 5, 1, to, at.c).start()

    def phase3(self, both, sums=False, deep=False):
        at, py = self.at, self.py
        width = py + 2
        wait_for(self.r8, self.recv.at[1])
        count = 3 * at.lines
        held = self.r8[...].reshape((count,) + self.r8.shape[2:])
        both[pl.ds(0, count)] = held
        turned = jnp.dot(flat(held), self.turn[...], preferred_element_type=F32)
        both[pl.ds(count, count)] = turned.astype(BF16).reshape(held.shape)
        cut = self.r8.shape[2]
        lanes = lane_ids(cut)

        def take(d, e):
            index = self.sel[d * 12 + e]
            value = both[jnp.maximum(index, 0)].astype(F32)
            return jnp.where(index >= 0, value, 0.0)

        def shift(value, by):
            return pltpu.roll(value, by % LANES, 1)

        base = jnp.zeros((cut, LANES), F32)
        if sums:
            gathered = self.r8[0, 2].astype(F32)
            for i in range(1, at.lines):
                gathered = gathered + self.r8[i, 2].astype(F32)
            gathered = shift(gathered, 2 * width - py)
            base = jnp.where((lanes >= 2 * width) & (lanes < 2 * width + 6 * at.lines), gathered, 0.0)

        def partial(d, dst):
            dst[0] = take(d, 0).astype(BF16)
            dst[1] = take(d, 1).astype(BF16)
            tile = base
            left = shift(take(d, 2), 1 + py)
            tile = jnp.where((lanes >= 1) & (lanes <= py), left, tile)
            right = shift(take(d, 3), width + 1)
            tile = jnp.where((lanes > width) & (lanes <= width + py), right, tile)
            for e, lane in ((4, 0), (5, width), (6, py + 1), (7, width + py + 1)):
                value = take(d, e + 4 if deep else e)
                tile = jnp.where(lanes == lane, shift(value, lane), tile)
                if deep:
                    beside = 2 * width + e - 4
                    tile = jnp.where(lanes == beside, shift(value, beside - 1), tile)
            dst[2] = tile.astype(BF16)

        slot = at.z * 2 + at.k
        for d in reversed(range(1, 2 * at.nz)):
            partial(d, self.p3src.at[d - 1])
            self.remote(self.p3src.at[d - 1], self.p3.at[slot], 6, 2, at.z_peer(d), at.c).start()
        partial(0, self.p3.at[slot])

    def halo_sum(self):
        wait_for(self.p3.at[pl.ds(0, 2 * self.at.nz - 1)], self.recv.at[2])
        total = {}
        for p in range(3):
            for a in range(self.a):
                total[p, a] = self.p3[a, p].astype(F32)
                for z in range(1, self.at.nz):
                    total[p, a] = total[p, a] + self.p3[2 * z + a, p].astype(F32)
        return total

    def phase4(self, total, extra=None):
        at, ranks = self.at, self.at.ranks
        for p in range(3):
            for a in range(self.a):
                self.h[p, a] = total[p, a].astype(BF16)
            if extra is not None:
                self.h[p, self.a] = extra[p].astype(BF16)
        self.local(self.h.at[2], self.cols.at[at.c], 5).start()
        for d in range(1, ranks):
            to = at.chan_peer(d)
            self.remote(self.h.at[2], self.cols.at[at.c], 7, 5, at.t, to).start()
        for side, rank, buf, bufx, sem in ((0, 0, self.up, self.upx, 3), (1, ranks - 1, self.dn, self.dnx, 4)):
            pieces = [(self.h.at[side, a], buf.at[a, at.c], 8 + side, sem) for a in range(self.a)]
            if self.extra:
                pieces.append((self.h.at[side, self.a], bufx.at[at.c], 8 + side, sem + 3))

            @pl.when(at.c == rank)
            def _():
                for src, dst, _, recv in pieces:
                    self.local(src, dst, recv).start()

            @pl.when(at.c != rank)
            def _():
                for src, dst, send, recv in pieces:
                    self.remote(src, dst, send, recv, at.t, rank).start()

    def finish(self):
        at = self.at
        wait_for(self.up, self.recv.at[3])
        wait_for(self.dn, self.recv.at[4])
        wait_for(self.cols, self.recv.at[5])
        if self.extra:

            @pl.when(at.c == 0)
            def _():
                wait_for(self.upx, self.recv.at[6])

            @pl.when(at.c == at.ranks - 1)
            def _():
                wait_for(self.dnx, self.recv.at[7])

    def slab_cols(self, a):
        value = flat(self.cols[:, a]).astype(F32)
        return pltpu.roll(value, lax.rem(LANES - ROWS * self.at.c, LANES), 1)

    def drain(self):
        at, ranks = self.at, self.at.ranks
        wait_for(self.p1.at[pl.ds(0, ranks - 1)], self.send.at[0])
        wait_for(self.r8.at[pl.ds(0, at.lines - 1)], self.send.at[5])
        wait_for(self.p3.at[pl.ds(0, 2 * at.nz - 1)], self.send.at[6])
        wait_for(self.cols.at[pl.ds(0, ranks - 1)], self.send.at[7])

        @pl.when(at.c == 0)
        def _():
            wait_for(self.p1.at[pl.ds(0, ranks - 1)], self.send.at[1])

        @pl.when(at.c == ranks - 1)
        def _():
            wait_for(self.p1.at[pl.ds(0, ranks - 1)], self.send.at[2])

        @pl.when(at.c < ranks - 1)
        def _():
            wait_for(self.up, self.send.at[3])
            wait_for(self.h.at[1], self.send.at[9])

        @pl.when(at.c > 0)
        def _():
            wait_for(self.dn, self.send.at[4])
            wait_for(self.h.at[0], self.send.at[8])


def round_scratch(a, a4, nx, nz, ranks, cut):
    vm = lambda *shape: pltpu.VMEM(shape + (cut, LANES), BF16)
    return [
        vm(ranks, a),
        vm(ranks + 2, a),
        vm(a, 3),
        vm(2 * nx, 3),
        vm(2 * nz - 1, 3),
        vm(2 * nz, 3),
        vm(3, a4),
        vm(a, ranks),
        vm(a, ranks),
        vm(ranks, a4),
        vm(ranks),
        vm(ranks),
        pltpu.SemaphoreType.DMA((10,)),
        pltpu.SemaphoreType.DMA((8,)),
    ]


ROUND_REFS = 14


def put_rows(stack, rows, cols, left_lane, right_lane, slots=None):
    lanes = lane_ids(LANES)
    for q, row in enumerate(rows):
        wide = row.astype(F32)
        here = pl.ds((q if slots is None else slots[q]) * LANES, LANES)
        first, last = left_lane + q, right_lane + q
        left = jnp.where(lanes == 0, cols[:, first : first + 1], pltpu.roll(wide, 1, 1))
        right = jnp.where(lanes == LANES - 1, cols[:, last : last + 1], pltpu.roll(wide, LANES - 1, 1))
        stack[pl.ds(0, LANES), here] = left.astype(BF16)
        stack[pl.ds(LANES, LANES), here] = row.astype(BF16)
        stack[pl.ds(2 * LANES, LANES), here] = right.astype(BF16)


def deep_cols(rnd, at, rows, py):
    width = py + 2
    lanes = lane_ids(LANES)
    near, far = flat(rnd.cols[:, 0]).astype(F32), flat(rnd.cols[:, 1]).astype(F32)

    def place(value):
        left = pltpu.roll(value, lax.rem(2 * LANES + 1 - ROWS * at.c, LANES), 1)
        right = pltpu.roll(value, lax.rem(2 * LANES + HALF + 1 - width - ROWS * at.c, LANES), 1)
        return jnp.where(lanes < HALF, left, right)

    one, two = place(near), place(far)
    top, bottom = at.c == 0, at.c == at.ranks - 1

    def put(tile, lane, value, source, where):
        return jnp.where(lanes == jnp.where(where, lane, -1), value[:, source : source + 1], tile)

    beside = 2 * width
    for base, corner, other in ((0, 0, py + 1), (HALF, width, width + py + 1)):
        n = 0 if base == 0 else 1
        one = put(one, base, far, corner, top)
        one = put(one, base + 7, far, other, bottom)
        two = put(two, base, far, beside + n, top)
        two = put(two, base + 1, near, beside + n, top)
        two = put(two, base + 6, near, beside + 2 + n, bottom)
        two = put(two, base + 7, far, beside + 2 + n, bottom)
    zero = jnp.zeros((LANES, LANES), F32)
    for q, row in enumerate(rows):
        wide = row.astype(F32)
        zero = jnp.where(lanes == q, wide[:, 0:1], zero)
        zero = jnp.where(lanes == HALF + q, wide[:, LANES - 1 :], zero)
    return zero, one, two


def edge_stack(edge, rows, cols, open_vertex):
    zero, one, two = cols
    lanes = lane_ids(LANES)
    hide = lambda tile, lane, n: jnp.where(lanes == jnp.where(open_vertex[n], lane, -1), 0.0, tile)
    upper = hide(hide(one, 2, 0), HALF + 2, 1)
    lower = hide(hide(one, 5, 2), HALF + 5, 3)
    put_rows(edge, rows[:3], upper, 0, HALF, (0, 3, 6))
    put_rows(edge, rows[5:], lower, 5, HALF + 5, (1, 4, 7))
    sides = (
        jnp.where(lanes < HALF, two, zero),
        one,
        jnp.where(lanes < HALF, zero, two),
    )
    for a in range(3):
        for b in range(3):
            tile = pltpu.roll(sides[b], LANES - a, 1) if a else sides[b]
            if a == 0 and b == 2:
                tile = hide(tile, 1, 0)
            if a == 0 and b == 0:
                tile = hide(tile, HALF + 1, 1)
            if a == 2 and b == 2:
                tile = hide(tile, 4, 2)
            if a == 2 and b == 0:
                tile = hide(tile, HALF + 4, 3)
            edge[pl.ds(b * LANES, LANES), pl.ds((3 * a + 2) * LANES, LANES)] = tile.astype(BF16)


def conv_rows(stack, weight, row, gates=None):
    summed = None
    for a in range(3):
        term = jnp.dot(
            weight(a), stack[:, pl.ds((row + a) * LANES, 2 * LANES)], preferred_element_type=F32
        )
        summed = term if summed is None else summed + term
    return summed


def kernel(dims, *refs):
    nx, nz, ranks, py = dims
    names = (
        "field", "hidden", "seam", "code", "corner", "cell", "pair", "enc_w", "gi_w", "gh_w", "dec_w",
        "mix_w", "enc_b", "gru_b", "gain", "shift", "dec_b", "state_out", "memory_out",
    )
    r = dict(zip(names, refs))
    given = dict(r)
    scratch = list(refs[len(names) :])
    take = lambda n: [scratch.pop(0) for _ in range(n)]
    (we, wi, wh, wdl, wdm, s_state, s_mem, s_enc, s_lift, s_edge, gh, both, sel, wsem, vec) = take(15)
    mems, coarses, states = take(2), take(2), take(1)
    field, hidden, turn = take(3)
    loaded = ("field", "hidden", "seam", "code", "corner", "cell", "pair", "mix_w", "enc_b", "gru_b", "gain", "shift", "dec_b")
    held = take(len(loaded))
    (lsem,) = take(1)
    round_refs = [take(ROUND_REFS) for _ in range(5)]
    width = py + 2
    cut = LANES // ranks
    lanes = lane_ids(LANES)
    column = lambda j: vec[:, j : j + 1]

    at = Place(nx, nz, ranks)

    barrier = pltpu.get_barrier_semaphore()
    peers = [(at.t, at.chan_peer(d)) for d in range(1, ranks)]
    peers += [(at.line_peer(d), at.c) for d in range(1, at.lines)]
    peers += [(at.z_peer(d), at.c) for d in range(2, 2 * nz)]
    for peer in peers:
        pl.semaphore_signal(barrier, inc=1, device_id=peer, device_id_type=MESH)

    copies = []
    for tap in range(9):
        a, lane = tap // 3, pl.ds(tap % 3 * LANES, LANES)
        copies += [
            pltpu.make_async_copy(r["enc_w"].at[tap], we.at[a, pl.ds(0, LANES), lane], wsem.at[0]),
            pltpu.make_async_copy(r["enc_w"].at[8 - tap], we.at[a, pl.ds(LANES, LANES), lane], wsem.at[0]),
            pltpu.make_async_copy(r["gi_w"].at[tap], wi.at[a, :, :, lane], wsem.at[1]),
            pltpu.make_async_copy(r["gh_w"].at[tap], wh.at[a, :, :, lane], wsem.at[2]),
            pltpu.make_async_copy(r["dec_w"].at[tap, :, pl.ds(0, LANES)], wdl.at[a, :, lane], wsem.at[3]),
            pltpu.make_async_copy(
                r["dec_w"].at[tap, :, pl.ds(LANES, LANES)], wdm.at[a, :, lane], wsem.at[4]
            ),
        ]
    loads = {}
    for n, name in enumerate(loaded):
        r[name] = held[n]
        loads[name] = pltpu.make_async_copy(given[name], held[n], lsem.at[n])
        loads[name].start()
    for copy in copies:
        copy.start()
    for name in loaded[2:7]:
        loads[name].wait()

    for d in range(2 * nz):
        dest = at.z_peer(d)
        for side in range(4):
            source = r["seam"][side, dest]
            code = r["code"][side, dest]
            sx, sz, sk = split_tile(jnp.maximum(source, 0), nz)
            piece = lax.div(code, 2) if side < 2 else 2
            index = (lax.rem(code, 2) * at.lines + sx * 2 + sk) * 3 + piece
            sel[d * 12 + side] = jnp.where((source >= 0) & (sz == at.z), index, -1)
        for corner in range(4):
            source = r["corner"][corner, dest]
            cell = r["cell"][corner, dest]
            sx, sz, sk = split_tile(jnp.maximum(source, 0), nz)
            flip = jnp.where(lax.rem(cell, LANES) > 0, 1, 0)
            index = (flip * at.lines + sx * 2 + sk) * 3 + lax.div(cell, LANES)
            sel[d * 12 + 4 + corner] = jnp.where((source >= 0) & (sz == at.z), index, -1)
            row_side, col_side = corner // 2, 2 + corner % 2
            near = r["seam"][row_side, dest]
            turned = lax.rem(r["code"][row_side, dest], 2)
            near_held = jnp.maximum(near, 0)
            hop = lambda table: jnp.where(
                turned == 1, r[table][5 - col_side, near_held], r[table][col_side, near_held]
            )
            source = hop("seam")
            turned = lax.rem(turned + lax.rem(hop("code"), 2), 2)
            theirs = jnp.where(turned == 1, corner, 3 - corner)
            sx, sz, sk = split_tile(jnp.maximum(source, 0), nz)
            index = (lax.rem(theirs, 2) * at.lines + sx * 2 + sk) * 3 + lax.div(theirs, 2)
            sel[d * 12 + 8 + corner] = jnp.where((near >= 0) & (source >= 0) & (sz == at.z), index, -1)

    for name, rows in (("field", field), ("hidden", hidden)):
        loads[name].wait()
        wide = r[name][...].astype(F32)
        for q in range(ROWS):
            rows[q] = wide[:, q, :].astype(BF16).reshape(rows.shape[1:])
    turn[...] = jnp.where(lanes + lax.broadcasted_iota(jnp.int32, (LANES, LANES), 0) == LANES - 1, 1.0, 0.0).astype(BF16)

    for name in loaded[7:]:
        loads[name].wait()
    gru_b = r["gru_b"]
    listed = [
        r["enc_b"][...], gru_b[0, 0:1] + gru_b[0, 1:2], gru_b[1, 0:1] + gru_b[1, 1:2], gru_b[2, 0:1],
        gru_b[2, 1:2], r["gain"][...], r["shift"][...], r["dec_b"][...],
    ]
    vec[...] = jnp.transpose(jnp.concatenate(listed + [jnp.zeros((LANES - 8, LANES), F32)], axis=0))

    def make_round(n, arrays, extra=False):
        return Round(at, round_refs[n], arrays, extra, sel, turn, py)

    def body_rows(rows, rnd, a):
        return [flat(rnd.up[a])] + [flat(rows[q]) for q in range(ROWS)] + [flat(rnd.dn[a])]

    def close_vertices(cols, left, right):
        for n, lane in enumerate((left, right, left + ROWS + 1, right + ROWS + 1)):
            cols = jnp.where(lanes == jnp.where(open_vertex[n], lane, -1), 0.0, cols)
        return cols

    def stack_rows(rows, rnd, a, stack, vertices=False):
        cols = rnd.slab_cols(a)
        if vertices:
            cols = close_vertices(cols, 0, width)
        put_rows(stack, body_rows(rows, rnd, a), cols, 0, width)

    first_rank, last_rank = at.c == 0, at.c == ranks - 1
    seams = [r["seam"][s, at.t] for s in range(4)]
    corners = [r["corner"][s, at.t] for s in range(4)]
    ranked = (first_rank, first_rank, last_rank, last_rank)
    odd = [lax.rem(r["code"][s, at.t], 2) == 1 for s in range(4)]
    turned_rows = (first_rank & odd[0], last_rank & odd[1])
    turned_cols = jnp.where(lanes < HALF, jnp.where(odd[2], 1, 0), jnp.where(odd[3], 1, 0))
    for n, (lane, cell) in enumerate(((0, 0), (HALF, LANES - 1), (ROWS + 1, LANES), (HALF + ROWS + 1, 2 * LANES - 1))):
        turned_here = jnp.where(r["cell"][n, at.t] == cell, 1, 0)
        turned_cols = jnp.where(lanes == jnp.where(ranked[n], lane, -1), turned_here, turned_cols)
    open_vertex = [rank & (corner < 0) for rank, corner in zip(ranked, corners)]

    def stack_state(rows, rnd):
        body = [flat(rnd.up[1])] + body_rows(rows, rnd, 0) + [flat(rnd.dn[1])]
        cols = deep_cols(rnd, at, body, py)
        put_rows(s_state, body[1:7], close_vertices(cols[1], 1, HALF + 1), 1, HALF + 1)
        edge_stack(s_edge, body, cols, open_vertex)

    def state_conv(gate):
        for n in range(2):
            gh[gate, :, pl.ds(2 * n * LANES, 2 * LANES)] = conv_rows(s_mem, lambda a: wh[a, gate], 2 * n)

    def encode():
        encoded = []
        for n in range(2):
            acc = gelu(conv_rows(s_state, lambda a: we[a, :LANES], 2 * n) + column(0)).astype(BF16)
            encoded += [acc[:, :LANES], acc[:, LANES:]]
        edge = None
        for a in range(3):
            term = jnp.dot(we[a], s_edge[:, pl.ds(3 * a * LANES, 3 * LANES)], preferred_element_type=F32)
            edge = term if edge is None else edge + term
        bias = column(0)
        pick = lambda n, there: gelu(
            jnp.where(there, edge[LANES:, n * LANES : (n + 1) * LANES], edge[:LANES, n * LANES : (n + 1) * LANES])
            + bias
        )
        above, below, beside = pick(0, turned_rows[0]), pick(1, turned_rows[1]), pick(2, turned_cols > 0)
        above = jnp.where(first_rank & (seams[0] < 0), 0.0, above).astype(BF16)
        below = jnp.where(last_rank & (seams[1] < 0), 0.0, below).astype(BF16)
        beside = jnp.where(lanes < jnp.where(seams[2] < 0, HALF, 0), 0.0, beside)
        beside = jnp.where(lanes >= jnp.where(seams[3] < 0, HALF, LANES), 0.0, beside)
        beside = close_vertices(beside, 0, HALF)
        put_rows(s_enc, [above] + encoded + [below], beside, 0, HALF)

    rounds = []
    rnd = make_round(0, [(field, 0), (field, 1)])
    late = make_round(4, [(hidden, 0), (hidden, 1)])
    rounds += [rnd, late]
    rnd.columns()
    late.columns()

    pl.semaphore_wait(barrier, len(peers))

    rnd.phase1()
    late.phase1()
    rnd.phase2()
    late.phase2()
    rnd.phase3(both, deep=True)
    late.phase3(both, deep=True)
    rnd.phase4(rnd.halo_sum())
    late.phase4(late.halo_sum())
    rnd.finish()
    stack_state(field, rnd)
    wait_for(we, wsem.at[0])
    encode()
    late.finish()
    stack_rows(hidden, late, 0, s_mem, True)
    wait_for(wh, wsem.at[2])
    for gate in range(3):
        state_conv(gate)
    wait_for(wi, wsem.at[1])
    state, memory = field, hidden

    for step in range(STEPS):
        if step > 0:
            encode()
        fresh = mems[step]
        coarse_rows = []
        for n in range(2):
            here = pl.ds(2 * n * LANES, 2 * LANES)
            gate = [conv_rows(s_enc, lambda a: wi[a, g], 2 * n) for g in range(3)]
            update = sigmoid(gate[0] + gh[0, :, here] + column(1))
            reset = sigmoid(gate[1] + gh[1, :, here] + column(2))
            candidate = jnp.tanh(gate[2] + column(3) + reset * (gh[2, :, here] + column(4)))
            pair = None
            for q in range(2):
                cut_row = slice(q * LANES, (q + 1) * LANES)
                before = flat(memory[2 * n + q]).astype(F32)
                after = (1.0 - update[:, cut_row]) * candidate[:, cut_row] + update[:, cut_row] * before
                after = after.astype(BF16)
                fresh[2 * n + q] = after.reshape(fresh.shape[1:])
                after = after.astype(F32)
                pair = after if pair is None else pair + after
            other = jnp.where(lax.rem(lanes, 2) == 0, pltpu.roll(pair, LANES - 1, 1), pltpu.roll(pair, 1, 1))
            coarse_rows.append((pair + other) * 0.25)
        coarse = coarses[step]
        for n in range(2):
            coarse[n] = coarse_rows[n].astype(BF16).reshape(coarse.shape[1:])
        sums = (
            0.5 * jnp.sum(coarse_rows[0] + coarse_rows[1], axis=1, keepdims=True),
            0.5
            * jnp.sum(
                coarse_rows[0] * coarse_rows[0] + coarse_rows[1] * coarse_rows[1], axis=1, keepdims=True
            ),
        )

        rnd = make_round(1 + 2 * step, [(fresh, 0), (coarse, 0)], extra=True)
        rounds.append(rnd)
        rnd.phase1(lambda: rnd.columns(sums))
        rnd.phase2(True)
        rnd.phase3(both, True)
        total = rnd.halo_sum()
        thin = lane_ids(cut)
        slice_here = pl.ds(pl.multiple_of(at.c * cut, cut), cut)
        gain, shift = vec[slice_here, 5:6], vec[slice_here, 6:7]

        def joint(tile):
            tile = jnp.maximum(tile, 0)
            picked = []
            for one in (tile, r["pair"][tile]):
                tx, tz, tk = split_tile(one, nz)
                lane = thin - (2 * width + 6 * (tx * 2 + tk))
                picked.append((rnd.p3[2 * tz + 1, 2].astype(F32), lane))
            result = []
            for low in (0, 3):
                masked = sum(
                    jnp.where((lane >= low) & (lane < low + 3), value, 0.0) for value, lane in picked
                )
                result.append(jnp.sum(masked, axis=1, keepdims=True))
            counted = 2 * (py // 2) * (LANES // 2)
            average = result[0] / counted
            spread = result[1] / counted - average * average
            return average, lax.rsqrt(spread + 1e-05)

        own = joint(at.t)
        stats = [joint(tile) for tile in seams + corners]

        def norm(value, average, scale):
            return gelu((value - average) * scale * gain + shift)

        extra = []
        for side in range(2):
            value = norm(total[side, 1], *stats[side])
            extra.append(jnp.where(seams[side] >= 0, value, 0.0))
        average = jnp.zeros((cut, LANES), F32)
        scale = jnp.zeros((cut, LANES), F32)
        valid = jnp.zeros((cut, LANES), F32)
        spans = ((2, 1, py), (3, width + 1, py), (4, 0, 1), (5, width, 1), (6, py + 1, 1), (7, width + py + 1, 1))
        for e, begin, length in spans:
            inside = (thin >= begin) & (thin < begin + length)
            average = jnp.where(inside, stats[e][0], average)
            scale = jnp.where(inside, stats[e][1], scale)
            flag = jnp.where((seams + corners)[e] >= 0, 1.0, 0.0)
            valid = jnp.where(inside, flag, valid)
        extra.append(jnp.where(valid > 0.0, norm(total[2, 1], average, scale), 0.0))
        colour = total[2, 1]
        for j, part in enumerate(three_parts(own[0]) + three_parts(own[1])):
            colour = jnp.where(thin == 2 * width + j, part, colour)
        total[2, 1] = colour
        rnd.phase4(total, extra)
        rnd.finish()

        raw = flat(rnd.cols[:, 1]).astype(F32)
        stat_lane = lanes - 2 * width
        mean = jnp.sum(jnp.where((stat_lane >= 0) & (stat_lane < 3), raw, 0.0), axis=1, keepdims=True)
        inverse = jnp.sum(jnp.where((stat_lane >= 3) & (stat_lane < 6), raw, 0.0), axis=1, keepdims=True)
        wide = lambda value: gelu((value - mean) * inverse * column(5) + column(6))
        top, bottom = flat(rnd.up[1]).astype(F32), flat(rnd.dn[1]).astype(F32)
        active = [
            jnp.where(first_rank, flat(rnd.upx[...]).astype(F32), wide(top)),
            wide(coarse_rows[0]),
            wide(coarse_rows[1]),
            jnp.where(last_rank, flat(rnd.dnx[...]).astype(F32), wide(bottom)),
            rnd.slab_cols(2),
        ]
        base = [top, coarse_rows[0], coarse_rows[1], bottom, rnd.slab_cols(1)]
        lifted = [
            (b + jnp.dot(r["mix_w"][...], v.astype(BF16), preferred_element_type=F32)).astype(BF16)
            for b, v in zip(base, active)
        ]
        body = [lifted[0], lifted[1], lifted[1], lifted[2], lifted[2], lifted[3]]
        put_rows(s_lift, body, lifted[4].astype(F32), 0, width)
        stack_rows(fresh, rnd, 0, s_mem)

        if step == 0:
            wait_for(wdl, wsem.at[3])
            wait_for(wdm, wsem.at[4])
        result = r["state_out"] if step == STEPS - 1 else states[step]
        for n in range(2):
            acc = conv_rows(s_lift, lambda a: wdl[a], 2 * n) + conv_rows(s_mem, lambda a: wdm[a], 2 * n)
            acc = acc + column(7)
            for q in range(2):
                before = flat(state[2 * n + q]).astype(F32)
                after = (before + acc[:, q * LANES : (q + 1) * LANES]).astype(BF16)
                result[2 * n + q] = after.reshape(result.shape[1:])
        state, memory = result, fresh
        if step < STEPS - 1:
            rnd = make_round(2 + 2 * step, [(state, 0), (state, 1)])
            rounds.append(rnd)
            rnd.phase1(rnd.columns)
            state_conv(0)
            rnd.phase2()
            state_conv(1)
            rnd.phase3(both, deep=True)
            state_conv(2)
            rnd.phase4(rnd.halo_sum())
            rnd.finish()
            stack_state(state, rnd)

    r["memory_out"][...] = memory[...]
    for rnd in rounds:
        rnd.drain()


def on_device(
    nx, nz, ranks, py,
    field, hidden_fine, seam_tile, seam_code, corner_tile, corner_cell, pair_list, enc_weight, enc_bias,
    gru_input, gru_state, gru_bias, coarse_gain, coarse_shift, coarse_weight, dec_weight, dec_bias,
):
    cut = LANES // ranks
    vmem, anywhere = (pl.BlockSpec(memory_space=s) for s in (pltpu.VMEM, pl.ANY))
    slab = (ROWS, ranks, cut, LANES)
    scratch = [
        pltpu.VMEM((3, 2 * LANES, 3 * LANES), BF16),
        pltpu.VMEM((3, 3, LANES, 3 * LANES), BF16),
        pltpu.VMEM((3, 3, LANES, 3 * LANES), BF16),
        pltpu.VMEM((3, LANES, 3 * LANES), BF16),
        pltpu.VMEM((3, LANES, 3 * LANES), BF16),
    ]
    scratch += [pltpu.VMEM((3 * LANES, 6 * LANES), BF16) for _ in range(4)]
    scratch += [pltpu.VMEM((3 * LANES, 9 * LANES), BF16)]
    scratch += [
        pltpu.VMEM((3, LANES, ROWS * LANES), F32),
        pltpu.VMEM((2 * 3 * 2 * nx, cut, LANES), BF16),
        pltpu.SMEM((2 * nz * 12,), jnp.int32),
        pltpu.SemaphoreType.DMA((5,)),
        pltpu.VMEM((LANES, LANES), F32),
    ]
    scratch += [pltpu.VMEM(slab, BF16) for _ in range(2)]
    scratch += [pltpu.VMEM((2, ranks, cut, LANES), BF16) for _ in range(2)]
    scratch += [pltpu.VMEM(slab, BF16) for _ in range(3)] + [pltpu.VMEM((LANES, LANES), BF16)]
    scratch += [pltpu.VMEM((LANES, ROWS, LANES), BF16)] * 2
    scratch += [pltpu.SMEM((4, seam_tile.shape[0]), jnp.int32)] * 4 + [pltpu.SMEM(pair_list.shape, jnp.int32)]
    scratch += [pltpu.VMEM((LANES, LANES), BF16), pltpu.VMEM((1, LANES), F32), pltpu.VMEM((3, 2, LANES), F32)]
    scratch += [pltpu.VMEM((1, LANES), F32)] * 3 + [pltpu.SemaphoreType.DMA((13,))]
    for a, a4 in ((2, 2), (2, 3), (2, 2), (2, 3), (2, 2)):
        scratch += round_scratch(a, a4, nx, nz, ranks, cut)
    state, memory = pl.pallas_call(
        functools.partial(kernel, (nx, nz, ranks, py)),
        out_shape=[jax.ShapeDtypeStruct(slab, BF16)] * 2,
        in_specs=[anywhere] * 17,
        out_specs=[vmem] * 2,
        scratch_shapes=scratch,
        compiler_params=pltpu.CompilerParams(
            collective_id=0, has_side_effects=True, vmem_limit_bytes=60 * 2**20
        ),
    )(
        field[:, 0], hidden_fine[:, 0], seam_tile.T, seam_code.T, corner_tile.T, corner_cell.T, pair_list,
        enc_weight, gru_input, gru_state, dec_weight, coarse_weight,
        enc_bias[None], jnp.transpose(gru_bias, (1, 0, 2)), coarse_gain[None], coarse_shift[None],
        dec_bias[None],
    )
    back = lambda v: jnp.transpose(v.reshape(ROWS, LANES, LANES), (1, 0, 2))[:, None]
    return back(state), back(memory)


def solution(mesh):
    ranks = mesh.shape["chan"]
    tiles = mesh.shape["tile"]
    nz = 4 if tiles == 32 else 2
    nx = tiles // (2 * nz)
    placed = (P(None, "tile", "chan", None),) * 2
    return jax.shard_map(
        functools.partial(on_device, nx, nz, ranks, ROWS * ranks),
        mesh=mesh,
        in_specs=placed + (P(),) * 15,
        out_specs=placed,
        check_vma=False,
    )
```

```python
import functools
import math

import jax
import jax.numpy as jnp
from jax import lax
from jax.experimental import pallas as pl
from jax.experimental.pallas import tpu as pltpu
from jax.sharding import PartitionSpec as P

STEPS = 2
LANES = 128
ROWS = 4
HALF = 64
F32 = jnp.float32
BF16 = jnp.bfloat16
MESH = pl.DeviceIdType.MESH


def gelu(x):
    inner = math.sqrt(2.0 / math.pi) * (x + 0.044715 * (x * x * x))
    return 0.5 * x * (1.0 + jnp.tanh(inner))


def sigmoid(x):
    return 0.5 + 0.5 * jnp.tanh(0.5 * x)


def flat(value):
    return value.reshape(-1, LANES)


def lane_ids(rows):
    return lax.broadcasted_iota(jnp.int32, (rows, LANES), 1)


def wait_for(ref, sem):
    pltpu.make_async_copy(ref, ref, sem).wait()


def three_parts(value):
    high = value.astype(BF16).astype(F32)
    rest = value - high
    middle = rest.astype(BF16).astype(F32)
    return high, middle, rest - middle


def split_tile(t, nz):
    return lax.div(t, 2 * nz), lax.rem(lax.div(t, 2), nz), lax.rem(t, 2)


class Place:
    def __init__(self, nx, nz, ranks):
        self.nx, self.nz, self.ranks = nx, nz, ranks
        self.t = lax.axis_index("tile")
        self.c = lax.axis_index("chan")
        self.x, self.z, self.k = split_tile(self.t, nz)
        self.i = self.x * 2 + self.k
        self.lines = 2 * nx

    def far_first(self):
        half = self.ranks // 2
        return sorted(range(1, self.ranks), key=lambda d: abs(d - half))

    def chan_peer(self, d):
        return lax.rem(self.c + d, self.ranks)

    def line_peer(self, d):
        other = lax.rem(self.i + d, self.lines)
        return lax.div(other, 2) * (2 * self.nz) + self.z * 2 + lax.rem(other, 2)

    def x_peer(self, dx, k):
        return lax.rem(self.x + dx, self.nx) * (2 * self.nz) + self.z * 2 + k

    def z_peer(self, d):
        z, k = lax.rem(self.z + d // 2, self.nz), lax.rem(self.k + d % 2, 2)
        return self.x * (2 * self.nz) + z * 2 + k


class Round:
    def __init__(self, at, refs, arrays, extra, sel, turn, py):
        (self.cols_src, self.p1, self.own, self.r8, self.p3src, self.p3, self.h,
         self.up, self.dn, self.cols, self.upx, self.dnx, self.send, self.recv) = refs
        self.at, self.arrays, self.extra, self.sel, self.turn, self.py = at, arrays, extra, sel, turn, py
        self.a = len(arrays)

    def remote(self, src, dst, send, recv, t, c):
        return pltpu.make_async_remote_copy(
            src_ref=src, dst_ref=dst, send_sem=self.send.at[send], recv_sem=self.recv.at[recv],
            device_id=(t, c), device_id_type=MESH,
        )

    def local(self, src, dst, recv):
        return pltpu.make_async_copy(src, dst, self.recv.at[recv])

    def columns(self, sums=None):
        at, py, ranks = self.at, self.py, self.at.ranks
        lanes = lane_ids(LANES)
        for a, (rows, deep) in enumerate(self.arrays):
            each = ROWS // rows.shape[0]
            tile = jnp.zeros((LANES, LANES), BF16)
            for q in range(ROWS):
                row = flat(rows[q // each])
                tile = jnp.where(lanes == q, row[:, deep : deep + 1], tile)
                tile = jnp.where(lanes == LANES - py + q, row[:, LANES - 1 - deep : LANES - deep], tile)
            tile = pltpu.roll(tile, ROWS * at.c, 1)
            if sums is not None and a == self.a - 1:
                parts = three_parts(sums[0]) + three_parts(sums[1])
                for j, part in enumerate(parts):
                    tile = jnp.where(lanes == py + 6 * at.c + j, part.astype(BF16), tile)
            self.cols_src[:, a] = tile.reshape(ranks, -1, LANES)

    def phase1(self, columns=None):
        at, ranks = self.at, self.at.ranks
        for a, (rows, deep) in enumerate(self.arrays):
            first, last = deep, rows.shape[0] - 1 - deep

            @pl.when(at.c < ranks - 1)
            def _():
                self.remote(rows.at[last], self.up.at[a], 3, 3, at.t, at.c + 1).start()

            @pl.when(at.c > 0)
            def _():
                self.remote(rows.at[first], self.dn.at[a], 4, 4, at.t, at.c - 1).start()

            @pl.when(at.c == 0)
            def _():
                self.local(rows.at[first, at.c], self.p1.at[ranks, a], 0).start()
                for d in range(1, ranks):
                    to = at.chan_peer(d)
                    self.remote(rows.at[first, to], self.p1.at[ranks, a], 1, 0, at.t, to).start()

            @pl.when(at.c == ranks - 1)
            def _():
                self.local(rows.at[last, at.c], self.p1.at[ranks + 1, a], 0).start()
                for d in range(1, ranks):
                    to = at.chan_peer(d)
                    self.remote(rows.at[last, to], self.p1.at[ranks + 1, a], 2, 0, at.t, to).start()

        if columns is not None:
            columns()
        self.local(self.cols_src.at[at.c], self.p1.at[at.c], 0).start()
        for d in at.far_first():
            to = at.chan_peer(d)
            self.remote(self.cols_src.at[to], self.p1.at[at.c], 0, 0, at.t, to).start()

    def phase2(self, sums=False):
        at, py, ranks = self.at, self.py, self.at.ranks
        wait_for(self.p1, self.recv.at[0])
        for a in range(self.a):
            self.own[a, 0] = self.p1[ranks, a]
            self.own[a, 1] = self.p1[ranks + 1, a]
            merged = self.p1[0, a]
            for r in range(1, ranks):
                merged = merged + self.p1[r, a]
            if sums and a == self.a - 1:
                merged = merged.astype(F32)
                lanes = lane_ids(merged.shape[0])
                held = (lanes >= py) & (lanes < py + 6 * ranks)
                kind = lax.rem(lanes - py + 6 * LANES, 6) < 3
                total = jnp.sum(jnp.where(held & kind, merged, 0.0), axis=1, keepdims=True)
                square = jnp.sum(
                    jnp.where(held & jnp.logical_not(kind), merged, 0.0), axis=1, keepdims=True
                )
                merged = jnp.where(held, 0.0, merged)
                parts = three_parts(total) + three_parts(square)
                for j, part in enumerate(parts):
                    merged = jnp.where(lanes == py + 6 * at.i + j, part, merged)
            self.own[a, 2] = merged.astype(BF16)
            for dx in sorted(range(1, at.nx), key=lambda d: abs(2 * d - at.nx)):
                self.remote(self.own.at[a], self.r8.at[at.i], 5, 1, at.x_peer(dx, a), at.c).start()

            @pl.when(at.k == a)
            def _():
                self.local(self.own.at[a], self.r8.at[at.i], 1).start()

            @pl.when(at.k != a)
            def _():
                self.remote(self.own.at[a], self.r8.at[at.i], 5, 1, at.x_peer(0, a), at.c).start()

    def phase3(self, both, sums=False, deep=False):
        at, py = self.at, self.py
        width = py + 2
        wait_for(self.r8, self.recv.at[1])
        count = 3 * at.lines
        held = self.r8[...].reshape((count,) + self.r8.shape[2:])
        both[pl.ds(0, count)] = held
        turned = jnp.dot(flat(held), self.turn[...], preferred_element_type=F32)
        both[pl.ds(count, count)] = turned.astype(BF16).reshape(held.shape)
        cut = self.r8.shape[2]
        lanes = lane_ids(cut)

        def take(d, e):
            index = self.sel[d * 12 + e]
            value = both[jnp.maximum(index, 0)]
            return jnp.where(index >= 0, value, jnp.zeros_like(value))

        def shift(value, by):
            return pltpu.roll(value, by % LANES, 1)

        base = jnp.zeros((cut, LANES), BF16)
        if sums:
            gathered = self.r8[0, 2]
            for i in range(1, at.lines):
                gathered = gathered + self.r8[i, 2]
            gathered = shift(gathered, 2 * width - py)
            base = jnp.where((lanes >= 2 * width) & (lanes < 2 * width + 6 * at.lines), gathered, base)

        def partial(d, dst):
            dst[0] = take(d, 0)
            dst[1] = take(d, 1)
            tile = base
            left = shift(take(d, 2), 1 + py)
            tile = jnp.where((lanes >= 1) & (lanes <= py), left, tile)
            right = shift(take(d, 3), width + 1)
            tile = jnp.where((lanes > width) & (lanes <= width + py), right, tile)
            for e, lane in ((4, 0), (5, width), (6, py + 1), (7, width + py + 1)):
                value = take(d, e + 4 if deep else e)
                tile = jnp.where(lanes == lane, shift(value, lane), tile)
                if deep:
                    beside = 2 * width + e - 4
                    tile = jnp.where(lanes == beside, shift(value, beside - 1), tile)
            dst[2] = tile

        slot = at.z * 2 + at.k
        for d in sorted(range(1, 2 * at.nz), key=lambda d: abs(2 * (d // 2) - at.nz)):
            partial(d, self.p3src.at[d - 1])
            self.remote(self.p3src.at[d - 1], self.p3.at[slot], 6, 2, at.z_peer(d), at.c).start()
        partial(0, self.p3.at[slot])

    def halo_sum(self):
        wait_for(self.p3.at[pl.ds(0, 2 * self.at.nz - 1)], self.recv.at[2])
        total = {}
        for p in range(3):
            for a in range(self.a):
                value = self.p3[a, p]
                for z in range(1, self.at.nz):
                    value = value + self.p3[2 * z + a, p]
                total[p, a] = value
        return total

    def phase4(self, total, extra=None):
        at, ranks = self.at, self.at.ranks
        for p in range(3):
            for a in range(self.a):
                self.h[p, a] = total[p, a].astype(BF16)
            if extra is not None:
                self.h[p, self.a] = extra[p].astype(BF16)
        for side, rank, buf, bufx, sem in ((0, 0, self.up, self.upx, 3), (1, ranks - 1, self.dn, self.dnx, 4)):
            pieces = [(self.h.at[side, a], buf.at[a, at.c], 8 + side, sem) for a in range(self.a)]
            if self.extra:
                pieces.append((self.h.at[side, self.a], bufx.at[at.c], 8 + side, sem + 3))

            @pl.when(at.c == rank)
            def _():
                for src, dst, _, recv in pieces:
                    self.local(src, dst, recv).start()

            @pl.when(at.c != rank)
            def _():
                for src, dst, send, recv in pieces:
                    self.remote(src, dst, send, recv, at.t, rank).start()

        self.local(self.h.at[2], self.cols.at[at.c], 5).start()
        for d in at.far_first():
            to = at.chan_peer(d)
            self.remote(self.h.at[2], self.cols.at[at.c], 7, 5, at.t, to).start()

    def finish(self):
        at = self.at
        wait_for(self.up, self.recv.at[3])
        wait_for(self.dn, self.recv.at[4])
        wait_for(self.cols, self.recv.at[5])
        if self.extra:

            @pl.when(at.c == 0)
            def _():
                wait_for(self.upx, self.recv.at[6])

            @pl.when(at.c == at.ranks - 1)
            def _():
                wait_for(self.dnx, self.recv.at[7])

    def slab_cols(self, a):
        value = flat(self.cols[:, a])
        return pltpu.roll(value, lax.rem(LANES - ROWS * self.at.c, LANES), 1)

    def drain(self):
        at, ranks = self.at, self.at.ranks
        wait_for(self.p1.at[pl.ds(0, ranks - 1)], self.send.at[0])
        wait_for(self.r8.at[pl.ds(0, at.lines - 1)], self.send.at[5])
        wait_for(self.p3.at[pl.ds(0, 2 * at.nz - 1)], self.send.at[6])
        wait_for(self.cols.at[pl.ds(0, ranks - 1)], self.send.at[7])

        @pl.when(at.c == 0)
        def _():
            wait_for(self.p1.at[pl.ds(0, ranks - 1)], self.send.at[1])

        @pl.when(at.c == ranks - 1)
        def _():
            wait_for(self.p1.at[pl.ds(0, ranks - 1)], self.send.at[2])

        @pl.when(at.c < ranks - 1)
        def _():
            wait_for(self.up, self.send.at[3])
            wait_for(self.h.at[1], self.send.at[9])

        @pl.when(at.c > 0)
        def _():
            wait_for(self.dn, self.send.at[4])
            wait_for(self.h.at[0], self.send.at[8])


def round_scratch(a, a4, nx, nz, ranks, cut):
    vm = lambda *shape: pltpu.VMEM(shape + (cut, LANES), BF16)
    return [
        vm(ranks, a),
        vm(ranks + 2, a),
        vm(a, 3),
        vm(2 * nx, 3),
        vm(2 * nz - 1, 3),
        vm(2 * nz, 3),
        vm(3, a4),
        vm(a, ranks),
        vm(a, ranks),
        vm(ranks, a4),
        vm(ranks),
        vm(ranks),
        pltpu.SemaphoreType.DMA((10,)),
        pltpu.SemaphoreType.DMA((8,)),
    ]


ROUND_REFS = 14


def put_rows(stack, rows, cols, left_lane, right_lane, slots=None):
    lanes = lane_ids(LANES)
    cols = cols.astype(BF16)
    held = {}
    for q, row in enumerate(rows):
        here = pl.ds((q if slots is None else slots[q]) * LANES, LANES)
        first, last = left_lane + q, right_lane + q
        if id(row) not in held:
            held[id(row)] = pltpu.roll(row, 1, 1), pltpu.roll(row, LANES - 1, 1)
        left, right = held[id(row)]
        stack[pl.ds(0, LANES), here] = jnp.where(lanes == 0, cols[:, first : first + 1], left)
        stack[pl.ds(LANES, LANES), here] = row
        stack[pl.ds(2 * LANES, LANES), here] = jnp.where(lanes == LANES - 1, cols[:, last : last + 1], right)


def deep_cols(rnd, at, rows, py):
    width = py + 2
    lanes = lane_ids(LANES)
    near, far = flat(rnd.cols[:, 0]), flat(rnd.cols[:, 1])

    def place(value):
        left = pltpu.roll(value, lax.rem(2 * LANES + 1 - ROWS * at.c, LANES), 1)
        right = pltpu.roll(value, lax.rem(2 * LANES + HALF + 1 - width - ROWS * at.c, LANES), 1)
        return jnp.where(lanes < HALF, left, right)

    one, two = place(near), place(far)
    top, bottom = at.c == 0, at.c == at.ranks - 1

    def put(tile, lane, value, source, where):
        return jnp.where(lanes == jnp.where(where, lane, -1), value[:, source : source + 1], tile)

    beside = 2 * width
    for base, corner, other in ((0, 0, py + 1), (HALF, width, width + py + 1)):
        n = 0 if base == 0 else 1
        one = put(one, base, far, corner, top)
        one = put(one, base + 7, far, other, bottom)
        two = put(two, base, far, beside + n, top)
        two = put(two, base + 1, near, beside + n, top)
        two = put(two, base + 6, near, beside + 2 + n, bottom)
        two = put(two, base + 7, far, beside + 2 + n, bottom)
    zero = jnp.zeros((LANES, LANES), BF16)
    for q, row in enumerate(rows):
        zero = jnp.where(lanes == q, row[:, 0:1], zero)
        zero = jnp.where(lanes == HALF + q, row[:, LANES - 1 :], zero)
    return zero, one, two


def edge_stack(edge, rows, cols, open_vertex):
    zero, one, two = cols
    lanes = lane_ids(LANES)
    hide = lambda tile, lane, n: jnp.where(lanes == jnp.where(open_vertex[n], lane, -1), jnp.zeros_like(tile), tile)
    upper = hide(hide(one, 2, 0), HALF + 2, 1)
    lower = hide(hide(one, 5, 2), HALF + 5, 3)
    put_rows(edge, rows[:3], upper, 0, HALF, (0, 3, 6))
    put_rows(edge, rows[5:], lower, 5, HALF + 5, (1, 4, 7))
    sides = (
        jnp.where(lanes < HALF, two, zero),
        one,
        jnp.where(lanes < HALF, zero, two),
    )
    for a in range(3):
        for b in range(3):
            tile = pltpu.roll(sides[b], LANES - a, 1) if a else sides[b]
            if a == 0 and b == 2:
                tile = hide(tile, 1, 0)
            if a == 0 and b == 0:
                tile = hide(tile, HALF + 1, 1)
            if a == 2 and b == 2:
                tile = hide(tile, 4, 2)
            if a == 2 and b == 0:
                tile = hide(tile, HALF + 4, 3)
            edge[pl.ds(b * LANES, LANES), pl.ds((3 * a + 2) * LANES, LANES)] = tile


def conv_rows(stack, weight, row, gates=None):
    summed = None
    for a in range(3):
        term = jnp.dot(
            weight(a), stack[:, pl.ds((row + a) * LANES, 2 * LANES)], preferred_element_type=F32
        )
        summed = term if summed is None else summed + term
    return summed


def kernel(dims, *refs):
    nx, nz, ranks, py = dims
    names = (
        "field", "hidden", "seam", "code", "corner", "cell", "pair", "enc_w", "gi_w", "gh_w", "dec_w",
        "mix_w", "enc_b", "gru_b", "gain", "shift", "dec_b", "state_out", "memory_out",
    )
    r = dict(zip(names, refs))
    given = dict(r)
    scratch = list(refs[len(names) :])
    take = lambda n: [scratch.pop(0) for _ in range(n)]
    (we, wi, wh, wdl, wdm, s_state, s_mem, s_enc, s_lift, s_edge, gh, both, sel, wsem, vec) = take(15)
    mems, coarses, states = take(2), take(2), take(1)
    field, hidden, turn = take(3)
    loaded = ("field", "hidden", "seam", "code", "corner", "cell", "pair", "mix_w", "enc_b", "gru_b", "gain", "shift", "dec_b")
    held = take(len(loaded))
    (lsem,) = take(1)
    round_refs = [take(ROUND_REFS) for _ in range(5)]
    width = py + 2
    cut = LANES // ranks
    lanes = lane_ids(LANES)
    column = lambda j: vec[:, j : j + 1]

    at = Place(nx, nz, ranks)

    barrier = pltpu.get_barrier_semaphore()
    peers = [(at.t, at.chan_peer(d)) for d in range(1, ranks)]
    peers += [(at.line_peer(d), at.c) for d in range(1, at.lines)]
    peers += [(at.z_peer(d), at.c) for d in range(2, 2 * nz)]
    for peer in peers:
        pl.semaphore_signal(barrier, inc=1, device_id=peer, device_id_type=MESH)

    copies = []
    for tap in range(9):
        a, lane = tap // 3, pl.ds(tap % 3 * LANES, LANES)
        copies += [
            pltpu.make_async_copy(r["enc_w"].at[tap], we.at[a, pl.ds(0, LANES), lane], wsem.at[0]),
            pltpu.make_async_copy(r["enc_w"].at[8 - tap], we.at[a, pl.ds(LANES, LANES), lane], wsem.at[0]),
            pltpu.make_async_copy(r["gi_w"].at[tap], wi.at[a, :, :, lane], wsem.at[1]),
            pltpu.make_async_copy(r["gh_w"].at[tap], wh.at[a, :, :, lane], wsem.at[2]),
            pltpu.make_async_copy(r["dec_w"].at[tap, :, pl.ds(0, LANES)], wdl.at[a, :, lane], wsem.at[3]),
            pltpu.make_async_copy(
                r["dec_w"].at[tap, :, pl.ds(LANES, LANES)], wdm.at[a, :, lane], wsem.at[4]
            ),
        ]
    loads = {}
    for n, name in enumerate(loaded):
        r[name] = held[n]
        loads[name] = pltpu.make_async_copy(given[name], held[n], lsem.at[n])
        loads[name].start()
    for copy in copies:
        copy.start()
    for name in loaded[2:7]:
        loads[name].wait()

    for d in range(2 * nz):
        dest = at.z_peer(d)
        for side in range(4):
            source = r["seam"][side, dest]
            code = r["code"][side, dest]
            sx, sz, sk = split_tile(jnp.maximum(source, 0), nz)
            piece = lax.div(code, 2) if side < 2 else 2
            index = (lax.rem(code, 2) * at.lines + sx * 2 + sk) * 3 + piece
            sel[d * 12 + side] = jnp.where((source >= 0) & (sz == at.z), index, -1)
        for corner in range(4):
            source = r["corner"][corner, dest]
            cell = r["cell"][corner, dest]
            sx, sz, sk = split_tile(jnp.maximum(source, 0), nz)
            flip = jnp.where(lax.rem(cell, LANES) > 0, 1, 0)
            index = (flip * at.lines + sx * 2 + sk) * 3 + lax.div(cell, LANES)
            sel[d * 12 + 4 + corner] = jnp.where((source >= 0) & (sz == at.z), index, -1)
            row_side, col_side = corner // 2, 2 + corner % 2
            near = r["seam"][row_side, dest]
            turned = lax.rem(r["code"][row_side, dest], 2)
            near_held = jnp.maximum(near, 0)
            hop = lambda table: jnp.where(
                turned == 1, r[table][5 - col_side, near_held], r[table][col_side, near_held]
            )
            source = hop("seam")
            turned = lax.rem(turned + lax.rem(hop("code"), 2), 2)
            theirs = jnp.where(turned == 1, corner, 3 - corner)
            sx, sz, sk = split_tile(jnp.maximum(source, 0), nz)
            index = (lax.rem(theirs, 2) * at.lines + sx * 2 + sk) * 3 + lax.div(theirs, 2)
            sel[d * 12 + 8 + corner] = jnp.where((near >= 0) & (source >= 0) & (sz == at.z), index, -1)

    for name, rows in (("field", field), ("hidden", hidden)):
        loads[name].wait()
        wide = r[name][...].astype(F32)
        for q in range(ROWS):
            rows[q] = wide[:, q, :].astype(BF16).reshape(rows.shape[1:])
    turn[...] = jnp.where(lanes + lax.broadcasted_iota(jnp.int32, (LANES, LANES), 0) == LANES - 1, 1.0, 0.0).astype(BF16)

    for name in loaded[7:]:
        loads[name].wait()
    gru_b = r["gru_b"]
    listed = [
        r["enc_b"][...], gru_b[0, 0:1] + gru_b[0, 1:2], gru_b[1, 0:1] + gru_b[1, 1:2], gru_b[2, 0:1],
        gru_b[2, 1:2], r["gain"][...], r["shift"][...], r["dec_b"][...],
    ]
    vec[...] = jnp.transpose(jnp.concatenate(listed + [jnp.zeros((LANES - 8, LANES), F32)], axis=0))

    def make_round(n, arrays, extra=False):
        return Round(at, round_refs[n], arrays, extra, sel, turn, py)

    def body_rows(rows, rnd, a):
        return [flat(rnd.up[a])] + [flat(rows[q]) for q in range(ROWS)] + [flat(rnd.dn[a])]

    def close_vertices(cols, left, right):
        for n, lane in enumerate((left, right, left + ROWS + 1, right + ROWS + 1)):
            cols = jnp.where(lanes == jnp.where(open_vertex[n], lane, -1), jnp.zeros_like(cols), cols)
        return cols

    def stack_rows(rows, rnd, a, stack, vertices=False):
        cols = rnd.slab_cols(a)
        if vertices:
            cols = close_vertices(cols, 0, width)
        put_rows(stack, body_rows(rows, rnd, a), cols, 0, width)

    first_rank, last_rank = at.c == 0, at.c == ranks - 1
    seams = [r["seam"][s, at.t] for s in range(4)]
    corners = [r["corner"][s, at.t] for s in range(4)]
    ranked = (first_rank, first_rank, last_rank, last_rank)
    odd = [lax.rem(r["code"][s, at.t], 2) == 1 for s in range(4)]
    turned_rows = (first_rank & odd[0], last_rank & odd[1])
    turned_cols = jnp.where(lanes < HALF, jnp.where(odd[2], 1, 0), jnp.where(odd[3], 1, 0))
    for n, (lane, cell) in enumerate(((0, 0), (HALF, LANES - 1), (ROWS + 1, LANES), (HALF + ROWS + 1, 2 * LANES - 1))):
        turned_here = jnp.where(r["cell"][n, at.t] == cell, 1, 0)
        turned_cols = jnp.where(lanes == jnp.where(ranked[n], lane, -1), turned_here, turned_cols)
    open_vertex = [rank & (corner < 0) for rank, corner in zip(ranked, corners)]

    def stack_state(rows, rnd):
        body = [flat(rnd.up[1])] + body_rows(rows, rnd, 0) + [flat(rnd.dn[1])]
        cols = deep_cols(rnd, at, body, py)
        put_rows(s_state, body[1:7], close_vertices(cols[1], 1, HALF + 1), 1, HALF + 1)
        edge_stack(s_edge, body, cols, open_vertex)

    def state_conv(gate):
        for n in range(2):
            gh[gate, :, pl.ds(2 * n * LANES, 2 * LANES)] = conv_rows(s_mem, lambda a: wh[a, gate], 2 * n)

    def encode():
        encoded = []
        for n in range(2):
            acc = gelu(conv_rows(s_state, lambda a: we[a, :LANES], 2 * n) + column(0)).astype(BF16)
            encoded += [acc[:, :LANES], acc[:, LANES:]]
        edge = None
        for a in range(3):
            term = jnp.dot(we[a], s_edge[:, pl.ds(3 * a * LANES, 3 * LANES)], preferred_element_type=F32)
            edge = term if edge is None else edge + term
        bias = column(0)
        pick = lambda n, there: gelu(
            jnp.where(there, edge[LANES:, n * LANES : (n + 1) * LANES], edge[:LANES, n * LANES : (n + 1) * LANES])
            + bias
        )
        above, below, beside = pick(0, turned_rows[0]), pick(1, turned_rows[1]), pick(2, turned_cols > 0)
        above = jnp.where(first_rank & (seams[0] < 0), 0.0, above).astype(BF16)
        below = jnp.where(last_rank & (seams[1] < 0), 0.0, below).astype(BF16)
        beside = jnp.where(lanes < jnp.where(seams[2] < 0, HALF, 0), 0.0, beside)
        beside = jnp.where(lanes >= jnp.where(seams[3] < 0, HALF, LANES), 0.0, beside)
        beside = close_vertices(beside, 0, HALF)
        put_rows(s_enc, [above] + encoded + [below], beside, 0, HALF)

    rounds = []
    rnd = make_round(0, [(field, 0), (field, 1)])
    late = make_round(4, [(hidden, 0), (hidden, 1)])
    rounds += [rnd, late]
    rnd.columns()
    late.columns()

    pl.semaphore_wait(barrier, len(peers))

    rnd.phase1()
    late.phase1()
    rnd.phase2()
    late.phase2()
    rnd.phase3(both, deep=True)
    late.phase3(both, deep=True)
    rnd.phase4(rnd.halo_sum())
    late.phase4(late.halo_sum())
    rnd.finish()
    stack_state(field, rnd)
    wait_for(we, wsem.at[0])
    encode()
    late.finish()
    stack_rows(hidden, late, 0, s_mem, True)
    wait_for(wh, wsem.at[2])
    for gate in range(3):
        state_conv(gate)
    wait_for(wi, wsem.at[1])
    state, memory = field, hidden

    for step in range(STEPS):
        if step > 0:
            encode()
        fresh = mems[step]
        coarse_rows = []
        for n in range(2):
            here = pl.ds(2 * n * LANES, 2 * LANES)
            gate = [conv_rows(s_enc, lambda a: wi[a, g], 2 * n) for g in range(3)]
            update = sigmoid(gate[0] + gh[0, :, here] + column(1))
            reset = sigmoid(gate[1] + gh[1, :, here] + column(2))
            candidate = jnp.tanh(gate[2] + column(3) + reset * (gh[2, :, here] + column(4)))
            pair = None
            for q in range(2):
                cut_row = slice(q * LANES, (q + 1) * LANES)
                before = flat(memory[2 * n + q]).astype(F32)
                after = (1.0 - update[:, cut_row]) * candidate[:, cut_row] + update[:, cut_row] * before
                after = after.astype(BF16)
                fresh[2 * n + q] = after.reshape(fresh.shape[1:])
                after = after.astype(F32)
                pair = after if pair is None else pair + after
            other = jnp.where(lax.rem(lanes, 2) == 0, pltpu.roll(pair, LANES - 1, 1), pltpu.roll(pair, 1, 1))
            coarse_rows.append((pair + other) * 0.25)
        coarse = coarses[step]
        for n in range(2):
            coarse[n] = coarse_rows[n].astype(BF16).reshape(coarse.shape[1:])
        sums = (
            0.5 * jnp.sum(coarse_rows[0] + coarse_rows[1], axis=1, keepdims=True),
            0.5
            * jnp.sum(
                coarse_rows[0] * coarse_rows[0] + coarse_rows[1] * coarse_rows[1], axis=1, keepdims=True
            ),
        )

        rnd = make_round(1 + 2 * step, [(fresh, 0), (coarse, 0)], extra=True)
        rounds.append(rnd)
        rnd.phase1(lambda: rnd.columns(sums))
        rnd.phase2(True)
        rnd.phase3(both, True)
        total = rnd.halo_sum()
        thin = lane_ids(cut)
        slice_here = pl.ds(pl.multiple_of(at.c * cut, cut), cut)
        gain, shift = vec[slice_here, 5:6], vec[slice_here, 6:7]

        def joint(tile):
            tile = jnp.maximum(tile, 0)
            picked = []
            for one in (tile, r["pair"][tile]):
                tx, tz, tk = split_tile(one, nz)
                lane = thin - (2 * width + 6 * (tx * 2 + tk))
                picked.append((rnd.p3[2 * tz + 1, 2].astype(F32), lane))
            result = []
            for low in (0, 3):
                masked = sum(
                    jnp.where((lane >= low) & (lane < low + 3), value, 0.0) for value, lane in picked
                )
                result.append(jnp.sum(masked, axis=1, keepdims=True))
            counted = 2 * (py // 2) * (LANES // 2)
            average = result[0] / counted
            spread = result[1] / counted - average * average
            return average, lax.rsqrt(spread + 1e-05)

        own = joint(at.t)
        stats = [joint(tile) for tile in seams + corners]

        def norm(value, average, scale):
            return gelu((value - average) * scale * gain + shift)

        extra = []
        for side in range(2):
            value = norm(total[side, 1].astype(F32), *stats[side])
            extra.append(jnp.where(seams[side] >= 0, value, 0.0))
        average = jnp.zeros((cut, LANES), F32)
        scale = jnp.zeros((cut, LANES), F32)
        valid = jnp.zeros((cut, LANES), F32)
        spans = ((2, 1, py), (3, width + 1, py), (4, 0, 1), (5, width, 1), (6, py + 1, 1), (7, width + py + 1, 1))
        for e, begin, length in spans:
            inside = (thin >= begin) & (thin < begin + length)
            average = jnp.where(inside, stats[e][0], average)
            scale = jnp.where(inside, stats[e][1], scale)
            flag = jnp.where((seams + corners)[e] >= 0, 1.0, 0.0)
            valid = jnp.where(inside, flag, valid)
        extra.append(jnp.where(valid > 0.0, norm(total[2, 1].astype(F32), average, scale), 0.0))
        colour = total[2, 1]
        for j, part in enumerate(three_parts(own[0]) + three_parts(own[1])):
            colour = jnp.where(thin == 2 * width + j, part.astype(BF16), colour)
        total[2, 1] = colour
        rnd.phase4(total, extra)
        rnd.finish()

        raw = flat(rnd.cols[:, 1]).astype(F32)
        stat_lane = lanes - 2 * width
        mean = jnp.sum(jnp.where((stat_lane >= 0) & (stat_lane < 3), raw, 0.0), axis=1, keepdims=True)
        inverse = jnp.sum(jnp.where((stat_lane >= 3) & (stat_lane < 6), raw, 0.0), axis=1, keepdims=True)
        wide = lambda value: gelu((value - mean) * inverse * column(5) + column(6))
        top, bottom = flat(rnd.up[1]).astype(F32), flat(rnd.dn[1]).astype(F32)
        active = [
            jnp.where(first_rank, flat(rnd.upx[...]).astype(F32), wide(top)),
            wide(coarse_rows[0]),
            wide(coarse_rows[1]),
            jnp.where(last_rank, flat(rnd.dnx[...]).astype(F32), wide(bottom)),
            rnd.slab_cols(2).astype(F32),
        ]
        base = [top, coarse_rows[0], coarse_rows[1], bottom, rnd.slab_cols(1).astype(F32)]
        lifted = [
            (b + jnp.dot(r["mix_w"][...], v.astype(BF16), preferred_element_type=F32)).astype(BF16)
            for b, v in zip(base, active)
        ]
        body = [lifted[0], lifted[1], lifted[1], lifted[2], lifted[2], lifted[3]]
        put_rows(s_lift, body, lifted[4], 0, width)
        stack_rows(fresh, rnd, 0, s_mem)

        if step == 0:
            wait_for(wdl, wsem.at[3])
            wait_for(wdm, wsem.at[4])
        result = r["state_out"] if step == STEPS - 1 else states[step]
        for n in range(2):
            acc = conv_rows(s_lift, lambda a: wdl[a], 2 * n) + conv_rows(s_mem, lambda a: wdm[a], 2 * n)
            acc = acc + column(7)
            for q in range(2):
                before = flat(state[2 * n + q]).astype(F32)
                after = (before + acc[:, q * LANES : (q + 1) * LANES]).astype(BF16)
                result[2 * n + q] = after.reshape(result.shape[1:])
        state, memory = result, fresh
        if step < STEPS - 1:
            rnd = make_round(2 + 2 * step, [(state, 0), (state, 1)])
            rounds.append(rnd)
            rnd.phase1(rnd.columns)
            state_conv(0)
            rnd.phase2()
            state_conv(1)
            rnd.phase3(both, deep=True)
            state_conv(2)
            rnd.phase4(rnd.halo_sum())
            rnd.finish()
            stack_state(state, rnd)

    r["memory_out"][...] = memory[...]
    for rnd in rounds:
        rnd.drain()


def on_device(
    nx, nz, ranks, py,
    field, hidden_fine, seam_tile, seam_code, corner_tile, corner_cell, pair_list, enc_weight, enc_bias,
    gru_input, gru_state, gru_bias, coarse_gain, coarse_shift, coarse_weight, dec_weight, dec_bias,
):
    cut = LANES // ranks
    vmem, anywhere = (pl.BlockSpec(memory_space=s) for s in (pltpu.VMEM, pl.ANY))
    slab = (ROWS, ranks, cut, LANES)
    scratch = [
        pltpu.VMEM((3, 2 * LANES, 3 * LANES), BF16),
        pltpu.VMEM((3, 3, LANES, 3 * LANES), BF16),
        pltpu.VMEM((3, 3, LANES, 3 * LANES), BF16),
        pltpu.VMEM((3, LANES, 3 * LANES), BF16),
        pltpu.VMEM((3, LANES, 3 * LANES), BF16),
    ]
    scratch += [pltpu.VMEM((3 * LANES, 6 * LANES), BF16) for _ in range(4)]
    scratch += [pltpu.VMEM((3 * LANES, 9 * LANES), BF16)]
    scratch += [
        pltpu.VMEM((3, LANES, ROWS * LANES), F32),
        pltpu.VMEM((2 * 3 * 2 * nx, cut, LANES), BF16),
        pltpu.SMEM((2 * nz * 12,), jnp.int32),
        pltpu.SemaphoreType.DMA((5,)),
        pltpu.VMEM((LANES, LANES), F32),
    ]
    scratch += [pltpu.VMEM(slab, BF16) for _ in range(2)]
    scratch += [pltpu.VMEM((2, ranks, cut, LANES), BF16) for _ in range(2)]
    scratch += [pltpu.VMEM(slab, BF16) for _ in range(3)] + [pltpu.VMEM((LANES, LANES), BF16)]
    scratch += [pltpu.VMEM((LANES, ROWS, LANES), BF16)] * 2
    scratch += [pltpu.SMEM((4, seam_tile.shape[0]), jnp.int32)] * 4 + [pltpu.SMEM(pair_list.shape, jnp.int32)]
    scratch += [pltpu.VMEM((LANES, LANES), BF16), pltpu.VMEM((1, LANES), F32), pltpu.VMEM((3, 2, LANES), F32)]
    scratch += [pltpu.VMEM((1, LANES), F32)] * 3 + [pltpu.SemaphoreType.DMA((13,))]
    for a, a4 in ((2, 2), (2, 3), (2, 2), (2, 3), (2, 2)):
        scratch += round_scratch(a, a4, nx, nz, ranks, cut)
    state, memory = pl.pallas_call(
        functools.partial(kernel, (nx, nz, ranks, py)),
        out_shape=[jax.ShapeDtypeStruct(slab, BF16)] * 2,
        in_specs=[anywhere] * 17,
        out_specs=[vmem] * 2,
        scratch_shapes=scratch,
        compiler_params=pltpu.CompilerParams(
            collective_id=0, has_side_effects=True, vmem_limit_bytes=60 * 2**20
        ),
    )(
        field[:, 0], hidden_fine[:, 0], seam_tile.T, seam_code.T, corner_tile.T, corner_cell.T, pair_list,
        enc_weight, gru_input, gru_state, dec_weight, coarse_weight,
        enc_bias[None], jnp.transpose(gru_bias, (1, 0, 2)), coarse_gain[None], coarse_shift[None],
        dec_bias[None],
    )
    back = lambda v: jnp.transpose(v.reshape(ROWS, LANES, LANES), (1, 0, 2))[:, None]
    return back(state), back(memory)


def solution(mesh):
    ranks = mesh.shape["chan"]
    tiles = mesh.shape["tile"]
    nz = 4 if tiles == 32 else 2
    nx = tiles // (2 * nz)
    placed = (P(None, "tile", "chan", None),) * 2
    return jax.shard_map(
        functools.partial(on_device, nx, nz, ranks, ROWS * ranks),
        mesh=mesh,
        in_specs=placed + (P(),) * 15,
        out_specs=placed,
        check_vma=False,
    )
```

```python
import functools
import math

import jax
import jax.numpy as jnp
from jax import lax
from jax.experimental import pallas as pl
from jax.experimental.pallas import tpu as pltpu
from jax.sharding import PartitionSpec as P

STEPS = 2
LANES = 128
ROWS = 4
HALF = 64
F32 = jnp.float32
BF16 = jnp.bfloat16
MESH = pl.DeviceIdType.MESH


def gelu(x):
    inner = math.sqrt(2.0 / math.pi) * (x + 0.044715 * (x * x * x))
    return 0.5 * x * (1.0 + jnp.tanh(inner))


def sigmoid(x):
    return 0.5 + 0.5 * jnp.tanh(0.5 * x)


def flat(value):
    return value.reshape(-1, LANES)


def lane_ids(rows):
    return lax.broadcasted_iota(jnp.int32, (rows, LANES), 1)


def wait_for(ref, sem):
    pltpu.make_async_copy(ref, ref, sem).wait()


def three_parts(value):
    high = value.astype(BF16).astype(F32)
    rest = value - high
    middle = rest.astype(BF16).astype(F32)
    return high, middle, rest - middle


def split_tile(t, nz):
    return lax.div(t, 2 * nz), lax.rem(lax.div(t, 2), nz), lax.rem(t, 2)


class Place:
    def __init__(self, nx, nz, ranks):
        self.nx, self.nz, self.ranks = nx, nz, ranks
        self.t = lax.axis_index("tile")
        self.c = lax.axis_index("chan")
        self.x, self.z, self.k = split_tile(self.t, nz)
        self.i = self.x * 2 + self.k
        self.lines = 2 * nx

    def far_first(self):
        half = self.ranks // 2
        return sorted(range(1, self.ranks), key=lambda d: abs(d - half))

    def chan_peer(self, d):
        return lax.rem(self.c + d, self.ranks)

    def line_peer(self, d):
        other = lax.rem(self.i + d, self.lines)
        return lax.div(other, 2) * (2 * self.nz) + self.z * 2 + lax.rem(other, 2)

    def x_peer(self, dx, k):
        return lax.rem(self.x + dx, self.nx) * (2 * self.nz) + self.z * 2 + k

    def z_peer(self, d):
        z, k = lax.rem(self.z + d // 2, self.nz), lax.rem(self.k + d % 2, 2)
        return self.x * (2 * self.nz) + z * 2 + k


class Round:
    def __init__(self, at, refs, arrays, extra, sel, turn, py):
        (self.cols_src, self.p1, self.own, self.r8, self.p3src, self.p3, self.h,
         self.up, self.dn, self.cols, self.upx, self.dnx, self.send, self.recv) = refs
        self.at, self.arrays, self.extra, self.sel, self.turn, self.py = at, arrays, extra, sel, turn, py
        self.a = len(arrays)

    def remote(self, src, dst, send, recv, t, c):
        return pltpu.make_async_remote_copy(
            src_ref=src, dst_ref=dst, send_sem=self.send.at[send], recv_sem=self.recv.at[recv],
            device_id=(t, c), device_id_type=MESH,
        )

    def local(self, src, dst, recv):
        return pltpu.make_async_copy(src, dst, self.recv.at[recv])

    def columns(self, sums=None):
        at, py, ranks = self.at, self.py, self.at.ranks
        lanes = lane_ids(LANES)
        for a, (rows, deep) in enumerate(self.arrays):
            each = ROWS // rows.shape[0]
            tile = jnp.zeros((LANES, LANES), BF16)
            for q in range(ROWS):
                row = flat(rows[q // each])
                tile = jnp.where(lanes == q, row[:, deep : deep + 1], tile)
                tile = jnp.where(lanes == LANES - py + q, row[:, LANES - 1 - deep : LANES - deep], tile)
            tile = pltpu.roll(tile, ROWS * at.c, 1)
            if sums is not None and a == self.a - 1:
                parts = three_parts(sums[0]) + three_parts(sums[1])
                for j, part in enumerate(parts):
                    tile = jnp.where(lanes == py + 6 * at.c + j, part.astype(BF16), tile)
            self.cols_src[:, a] = tile.reshape(ranks, -1, LANES)

    def phase1(self, columns=None):
        at, ranks = self.at, self.at.ranks
        for a, (rows, deep) in enumerate(self.arrays):
            first, last = deep, rows.shape[0] - 1 - deep

            @pl.when(at.c < ranks - 1)
            def _():
                self.remote(rows.at[last], self.up.at[a], 3, 3, at.t, at.c + 1).start()

            @pl.when(at.c > 0)
            def _():
                self.remote(rows.at[first], self.dn.at[a], 4, 4, at.t, at.c - 1).start()

            @pl.when(at.c == 0)
            def _():
                self.local(rows.at[first, at.c], self.p1.at[ranks, a], 0).start()
                for d in range(1, ranks):
                    to = at.chan_peer(d)
                    self.remote(rows.at[first, to], self.p1.at[ranks, a], 1, 0, at.t, to).start()

            @pl.when(at.c == ranks - 1)
            def _():
                self.local(rows.at[last, at.c], self.p1.at[ranks + 1, a], 0).start()
                for d in range(1, ranks):
                    to = at.chan_peer(d)
                    self.remote(rows.at[last, to], self.p1.at[ranks + 1, a], 2, 0, at.t, to).start()

        if columns is not None:
            columns()
        self.local(self.cols_src.at[at.c], self.p1.at[at.c], 0).start()
        for d in at.far_first():
            to = at.chan_peer(d)
            self.remote(self.cols_src.at[to], self.p1.at[at.c], 0, 0, at.t, to).start()

    def phase2(self, sums=False):
        at, py, ranks = self.at, self.py, self.at.ranks
        wait_for(self.p1, self.recv.at[0])
        for a in range(self.a):
            self.own[a, 0] = self.p1[ranks, a]
            self.own[a, 1] = self.p1[ranks + 1, a]
            merged = self.p1[0, a]
            for r in range(1, ranks):
                merged = merged + self.p1[r, a]
            if sums and a == self.a - 1:
                merged = merged.astype(F32)
                lanes = lane_ids(merged.shape[0])
                held = (lanes >= py) & (lanes < py + 6 * ranks)
                kind = lax.rem(lanes - py + 6 * LANES, 6) < 3
                total = jnp.sum(jnp.where(held & kind, merged, 0.0), axis=1, keepdims=True)
                square = jnp.sum(
                    jnp.where(held & jnp.logical_not(kind), merged, 0.0), axis=1, keepdims=True
                )
                merged = jnp.where(held, 0.0, merged)
                parts = three_parts(total) + three_parts(square)
                for j, part in enumerate(parts):
                    merged = jnp.where(lanes == py + 6 * at.i + j, part, merged)
            self.own[a, 2] = merged.astype(BF16)
            for dx in sorted(range(1, at.nx), key=lambda d: abs(2 * d - at.nx)):
                self.remote(self.own.at[a], self.r8.at[at.i], 5, 1, at.x_peer(dx, a), at.c).start()

            @pl.when(at.k == a)
            def _():
                self.local(self.own.at[a], self.r8.at[at.i], 1).start()

            @pl.when(at.k != a)
            def _():
                self.remote(self.own.at[a], self.r8.at[at.i], 5, 1, at.x_peer(0, a), at.c).start()

    def phase3(self, both, sums=False, deep=False):
        at, py = self.at, self.py
        width = py + 2
        wait_for(self.r8, self.recv.at[1])
        count = 3 * at.lines
        held = self.r8[...].reshape((count,) + self.r8.shape[2:])
        both[pl.ds(0, count)] = held
        turned = jnp.dot(flat(held), self.turn[...], preferred_element_type=F32)
        both[pl.ds(count, count)] = turned.astype(BF16).reshape(held.shape)
        cut = self.r8.shape[2]
        lanes = lane_ids(cut)

        def take(d, e):
            index = self.sel[d * 12 + e]
            value = both[jnp.maximum(index, 0)]
            return jnp.where(index >= 0, value, jnp.zeros_like(value))

        def shift(value, by):
            return pltpu.roll(value, by % LANES, 1)

        base = jnp.zeros((cut, LANES), BF16)
        if sums:
            gathered = self.r8[0, 2]
            for i in range(1, at.lines):
                gathered = gathered + self.r8[i, 2]
            gathered = shift(gathered, 2 * width - py)
            base = jnp.where((lanes >= 2 * width) & (lanes < 2 * width + 6 * at.lines), gathered, base)

        def partial(d, dst):
            dst[0] = take(d, 0)
            dst[1] = take(d, 1)
            tile = base
            left = shift(take(d, 2), 1 + py)
            tile = jnp.where((lanes >= 1) & (lanes <= py), left, tile)
            right = shift(take(d, 3), width + 1)
            tile = jnp.where((lanes > width) & (lanes <= width + py), right, tile)
            for e, lane in ((4, 0), (5, width), (6, py + 1), (7, width + py + 1)):
                value = take(d, e + 4 if deep else e)
                tile = jnp.where(lanes == lane, shift(value, lane), tile)
                if deep:
                    beside = 2 * width + e - 4
                    tile = jnp.where(lanes == beside, shift(value, beside - 1), tile)
            dst[2] = tile

        slot = at.z * 2 + at.k
        for d in sorted(range(1, 2 * at.nz), key=lambda d: abs(2 * (d // 2) - at.nz)):
            partial(d, self.p3src.at[d - 1])
            self.remote(self.p3src.at[d - 1], self.p3.at[slot], 6, 2, at.z_peer(d), at.c).start()
        partial(0, self.p3.at[slot])

    def halo_sum(self):
        wait_for(self.p3.at[pl.ds(0, 2 * self.at.nz - 1)], self.recv.at[2])
        total = {}
        for p in range(3):
            for a in range(self.a):
                value = self.p3[a, p]
                for z in range(1, self.at.nz):
                    value = value + self.p3[2 * z + a, p]
                total[p, a] = value
        return total

    def phase4(self, total, extra=None):
        at, ranks = self.at, self.at.ranks
        for p in range(3):
            for a in range(self.a):
                self.h[p, a] = total[p, a].astype(BF16)
            if extra is not None:
                self.h[p, self.a] = extra[p].astype(BF16)
        for side, rank, buf, bufx, sem in ((0, 0, self.up, self.upx, 3), (1, ranks - 1, self.dn, self.dnx, 4)):
            pieces = [(self.h.at[side, a], buf.at[a, at.c], 8 + side, sem) for a in range(self.a)]
            if self.extra:
                pieces.append((self.h.at[side, self.a], bufx.at[at.c], 8 + side, sem + 3))

            @pl.when(at.c == rank)
            def _():
                for src, dst, _, recv in pieces:
                    self.local(src, dst, recv).start()

            @pl.when(at.c != rank)
            def _():
                for src, dst, send, recv in pieces:
                    self.remote(src, dst, send, recv, at.t, rank).start()

        self.local(self.h.at[2], self.cols.at[at.c], 5).start()
        for d in at.far_first():
            to = at.chan_peer(d)
            self.remote(self.h.at[2], self.cols.at[at.c], 7, 5, at.t, to).start()

    def finish(self):
        at = self.at
        wait_for(self.up, self.recv.at[3])
        wait_for(self.dn, self.recv.at[4])
        wait_for(self.cols, self.recv.at[5])
        if self.extra:

            @pl.when(at.c == 0)
            def _():
                wait_for(self.upx, self.recv.at[6])

            @pl.when(at.c == at.ranks - 1)
            def _():
                wait_for(self.dnx, self.recv.at[7])

    def slab_cols(self, a):
        value = flat(self.cols[:, a])
        return pltpu.roll(value, lax.rem(LANES - ROWS * self.at.c, LANES), 1)

    def drain(self):
        at, ranks = self.at, self.at.ranks
        wait_for(self.p1.at[pl.ds(0, ranks - 1)], self.send.at[0])
        wait_for(self.r8.at[pl.ds(0, at.lines - 1)], self.send.at[5])
        wait_for(self.p3.at[pl.ds(0, 2 * at.nz - 1)], self.send.at[6])
        wait_for(self.cols.at[pl.ds(0, ranks - 1)], self.send.at[7])

        @pl.when(at.c == 0)
        def _():
            wait_for(self.p1.at[pl.ds(0, ranks - 1)], self.send.at[1])

        @pl.when(at.c == ranks - 1)
        def _():
            wait_for(self.p1.at[pl.ds(0, ranks - 1)], self.send.at[2])

        @pl.when(at.c < ranks - 1)
        def _():
            wait_for(self.up, self.send.at[3])
            wait_for(self.h.at[1], self.send.at[9])

        @pl.when(at.c > 0)
        def _():
            wait_for(self.dn, self.send.at[4])
            wait_for(self.h.at[0], self.send.at[8])


def round_scratch(a, a4, nx, nz, ranks, cut):
    vm = lambda *shape: pltpu.VMEM(shape + (cut, LANES), BF16)
    return [
        vm(ranks, a),
        vm(ranks + 2, a),
        vm(a, 3),
        vm(2 * nx, 3),
        vm(2 * nz - 1, 3),
        vm(2 * nz, 3),
        vm(3, a4),
        vm(a, ranks),
        vm(a, ranks),
        vm(ranks, a4),
        vm(ranks),
        vm(ranks),
        pltpu.SemaphoreType.DMA((10,)),
        pltpu.SemaphoreType.DMA((8,)),
    ]


ROUND_REFS = 14


def put_rows(stack, rows, cols, left_lane, right_lane, slots=None):
    lanes = lane_ids(LANES)
    cols = cols.astype(BF16)
    held = {}
    for q, row in enumerate(rows):
        here = pl.ds((q if slots is None else slots[q]) * LANES, LANES)
        first, last = left_lane + q, right_lane + q
        if id(row) not in held:
            held[id(row)] = pltpu.roll(row, 1, 1), pltpu.roll(row, LANES - 1, 1)
        left, right = held[id(row)]
        stack[pl.ds(0, LANES), here] = jnp.where(lanes == 0, cols[:, first : first + 1], left)
        stack[pl.ds(LANES, LANES), here] = row
        stack[pl.ds(2 * LANES, LANES), here] = jnp.where(lanes == LANES - 1, cols[:, last : last + 1], right)


def deep_cols(rnd, at, rows, py):
    width = py + 2
    lanes = lane_ids(LANES)
    near, far = flat(rnd.cols[:, 0]), flat(rnd.cols[:, 1])

    def place(value):
        left = pltpu.roll(value, lax.rem(2 * LANES + 1 - ROWS * at.c, LANES), 1)
        right = pltpu.roll(value, lax.rem(2 * LANES + HALF + 1 - width - ROWS * at.c, LANES), 1)
        return jnp.where(lanes < HALF, left, right)

    one, two = place(near), place(far)
    top, bottom = at.c == 0, at.c == at.ranks - 1

    def put(tile, lane, value, source, where):
        return jnp.where(lanes == jnp.where(where, lane, -1), value[:, source : source + 1], tile)

    beside = 2 * width
    for base, corner, other in ((0, 0, py + 1), (HALF, width, width + py + 1)):
        n = 0 if base == 0 else 1
        one = put(one, base, far, corner, top)
        one = put(one, base + 7, far, other, bottom)
        two = put(two, base, far, beside + n, top)
        two = put(two, base + 1, near, beside + n, top)
        two = put(two, base + 6, near, beside + 2 + n, bottom)
        two = put(two, base + 7, far, beside + 2 + n, bottom)
    zero = jnp.zeros((LANES, LANES), BF16)
    for q, row in enumerate(rows):
        zero = jnp.where(lanes == q, row[:, 0:1], zero)
        zero = jnp.where(lanes == HALF + q, row[:, LANES - 1 :], zero)
    return zero, one, two


def edge_stack(edge, rows, cols, open_vertex):
    zero, one, two = cols
    lanes = lane_ids(LANES)
    hide = lambda tile, lane, n: jnp.where(lanes == jnp.where(open_vertex[n], lane, -1), jnp.zeros_like(tile), tile)
    upper = hide(hide(one, 2, 0), HALF + 2, 1)
    lower = hide(hide(one, 5, 2), HALF + 5, 3)
    put_rows(edge, rows[:3], upper, 0, HALF, (0, 3, 6))
    put_rows(edge, rows[5:], lower, 5, HALF + 5, (1, 4, 7))
    sides = (
        jnp.where(lanes < HALF, two, zero),
        one,
        jnp.where(lanes < HALF, zero, two),
    )
    for a in range(3):
        for b in range(3):
            tile = pltpu.roll(sides[b], LANES - a, 1) if a else sides[b]
            if a == 0 and b == 2:
                tile = hide(tile, 1, 0)
            if a == 0 and b == 0:
                tile = hide(tile, HALF + 1, 1)
            if a == 2 and b == 2:
                tile = hide(tile, 4, 2)
            if a == 2 and b == 0:
                tile = hide(tile, HALF + 4, 3)
            edge[pl.ds(b * LANES, LANES), pl.ds((3 * a + 2) * LANES, LANES)] = tile


def conv_rows(stack, weight, row, gates=None):
    summed = None
    for a in range(3):
        term = jnp.dot(
            weight(a), stack[:, pl.ds((row + a) * LANES, 2 * LANES)], preferred_element_type=F32
        )
        summed = term if summed is None else summed + term
    return summed


def kernel(dims, *refs):
    nx, nz, ranks, py = dims
    names = (
        "field", "hidden", "seam", "code", "corner", "cell", "pair", "enc_w", "gi_w", "gh_w", "dec_w",
        "mix_w", "enc_b", "gru_b", "gain", "shift", "dec_b", "state_out", "memory_out",
    )
    r = dict(zip(names, refs))
    given = dict(r)
    scratch = list(refs[len(names) :])
    take = lambda n: [scratch.pop(0) for _ in range(n)]
    (we, wi, wh, wdl, wdm, s_state, s_mem, s_enc, s_lift, s_edge, gh, both, sel, wsem, vec) = take(15)
    mems, coarses, states = take(2), take(2), take(1)
    field, hidden, turn = take(3)
    loaded = ("field", "hidden", "seam", "code", "corner", "cell", "pair", "mix_w", "enc_b", "gru_b", "gain", "shift", "dec_b")
    held = take(len(loaded))
    (lsem,) = take(1)
    round_refs = [take(ROUND_REFS) for _ in range(5)]
    width = py + 2
    cut = LANES // ranks
    lanes = lane_ids(LANES)
    column = lambda j: vec[:, j : j + 1]

    at = Place(nx, nz, ranks)

    barrier = pltpu.get_barrier_semaphore()
    peers = [(at.t, at.chan_peer(d)) for d in range(1, ranks)]
    peers += [(at.line_peer(d), at.c) for d in range(1, at.lines)]
    peers += [(at.z_peer(d), at.c) for d in range(2, 2 * nz)]
    for peer in peers:
        pl.semaphore_signal(barrier, inc=1, device_id=peer, device_id_type=MESH)

    copies = []
    for tap in range(9):
        a, lane = tap // 3, pl.ds(tap % 3 * LANES, LANES)
        copies += [
            pltpu.make_async_copy(r["enc_w"].at[tap], we.at[a, pl.ds(0, LANES), lane], wsem.at[0]),
            pltpu.make_async_copy(r["enc_w"].at[8 - tap], we.at[a, pl.ds(LANES, LANES), lane], wsem.at[0]),
            pltpu.make_async_copy(r["gi_w"].at[tap], wi.at[a, :, :, lane], wsem.at[1]),
            pltpu.make_async_copy(r["gh_w"].at[tap], wh.at[a, :, :, lane], wsem.at[2]),
            pltpu.make_async_copy(r["dec_w"].at[tap, :, pl.ds(0, LANES)], wdl.at[a, :, lane], wsem.at[3]),
            pltpu.make_async_copy(
                r["dec_w"].at[tap, :, pl.ds(LANES, LANES)], wdm.at[a, :, lane], wsem.at[4]
            ),
        ]
    loads = {}
    for n, name in enumerate(loaded):
        r[name] = held[n]
        loads[name] = pltpu.make_async_copy(given[name], held[n], lsem.at[n])
        loads[name].start()
    for copy in copies:
        copy.start()
    for name in loaded[2:7]:
        loads[name].wait()

    for d in range(2 * nz):
        dest = at.z_peer(d)
        for side in range(4):
            source = r["seam"][side, dest]
            code = r["code"][side, dest]
            sx, sz, sk = split_tile(jnp.maximum(source, 0), nz)
            piece = lax.div(code, 2) if side < 2 else 2
            index = (lax.rem(code, 2) * at.lines + sx * 2 + sk) * 3 + piece
            sel[d * 12 + side] = jnp.where((source >= 0) & (sz == at.z), index, -1)
        for corner in range(4):
            source = r["corner"][corner, dest]
            cell = r["cell"][corner, dest]
            sx, sz, sk = split_tile(jnp.maximum(source, 0), nz)
            flip = jnp.where(lax.rem(cell, LANES) > 0, 1, 0)
            index = (flip * at.lines + sx * 2 + sk) * 3 + lax.div(cell, LANES)
            sel[d * 12 + 4 + corner] = jnp.where((source >= 0) & (sz == at.z), index, -1)
            row_side, col_side = corner // 2, 2 + corner % 2
            near = r["seam"][row_side, dest]
            turned = lax.rem(r["code"][row_side, dest], 2)
            near_held = jnp.maximum(near, 0)
            hop = lambda table: jnp.where(
                turned == 1, r[table][5 - col_side, near_held], r[table][col_side, near_held]
            )
            source = hop("seam")
            turned = lax.rem(turned + lax.rem(hop("code"), 2), 2)
            theirs = jnp.where(turned == 1, corner, 3 - corner)
            sx, sz, sk = split_tile(jnp.maximum(source, 0), nz)
            index = (lax.rem(theirs, 2) * at.lines + sx * 2 + sk) * 3 + lax.div(theirs, 2)
            sel[d * 12 + 8 + corner] = jnp.where((near >= 0) & (source >= 0) & (sz == at.z), index, -1)

    for name, rows in (("field", field), ("hidden", hidden)):
        loads[name].wait()
        wide = r[name][...].astype(F32)
        for q in range(ROWS):
            rows[q] = wide[:, q, :].astype(BF16).reshape(rows.shape[1:])
    turn[...] = jnp.where(lanes + lax.broadcasted_iota(jnp.int32, (LANES, LANES), 0) == LANES - 1, 1.0, 0.0).astype(BF16)

    for name in loaded[7:]:
        loads[name].wait()
    gru_b = r["gru_b"]
    listed = [
        r["enc_b"][...], gru_b[0, 0:1] + gru_b[0, 1:2], gru_b[1, 0:1] + gru_b[1, 1:2], gru_b[2, 0:1],
        gru_b[2, 1:2], r["gain"][...], r["shift"][...], r["dec_b"][...],
    ]
    vec[...] = jnp.transpose(jnp.concatenate(listed + [jnp.zeros((LANES - 8, LANES), F32)], axis=0))

    def make_round(n, arrays, extra=False):
        return Round(at, round_refs[n], arrays, extra, sel, turn, py)

    def body_rows(rows, rnd, a):
        return [flat(rnd.up[a])] + [flat(rows[q]) for q in range(ROWS)] + [flat(rnd.dn[a])]

    def close_vertices(cols, left, right):
        for n, lane in enumerate((left, right, left + ROWS + 1, right + ROWS + 1)):
            cols = jnp.where(lanes == jnp.where(open_vertex[n], lane, -1), jnp.zeros_like(cols), cols)
        return cols

    def stack_rows(rows, rnd, a, stack, vertices=False):
        cols = rnd.slab_cols(a)
        if vertices:
            cols = close_vertices(cols, 0, width)
        put_rows(stack, body_rows(rows, rnd, a), cols, 0, width)

    first_rank, last_rank = at.c == 0, at.c == ranks - 1
    seams = [r["seam"][s, at.t] for s in range(4)]
    corners = [r["corner"][s, at.t] for s in range(4)]
    ranked = (first_rank, first_rank, last_rank, last_rank)
    odd = [lax.rem(r["code"][s, at.t], 2) == 1 for s in range(4)]
    turned_rows = (first_rank & odd[0], last_rank & odd[1])
    turned_cols = jnp.where(lanes < HALF, jnp.where(odd[2], 1, 0), jnp.where(odd[3], 1, 0))
    for n, (lane, cell) in enumerate(((0, 0), (HALF, LANES - 1), (ROWS + 1, LANES), (HALF + ROWS + 1, 2 * LANES - 1))):
        turned_here = jnp.where(r["cell"][n, at.t] == cell, 1, 0)
        turned_cols = jnp.where(lanes == jnp.where(ranked[n], lane, -1), turned_here, turned_cols)
    open_vertex = [rank & (corner < 0) for rank, corner in zip(ranked, corners)]

    def stack_state(rows, rnd):
        body = [flat(rnd.up[1])] + body_rows(rows, rnd, 0) + [flat(rnd.dn[1])]
        cols = deep_cols(rnd, at, body, py)
        put_rows(s_state, body[1:7], close_vertices(cols[1], 1, HALF + 1), 1, HALF + 1)
        edge_stack(s_edge, body, cols, open_vertex)

    def state_conv(gate):
        for n in range(2):
            gh[gate, :, pl.ds(2 * n * LANES, 2 * LANES)] = conv_rows(s_mem, lambda a: wh[a, gate], 2 * n)

    def encode():
        encoded = []
        for n in range(2):
            acc = gelu(conv_rows(s_state, lambda a: we[a, :LANES], 2 * n) + column(0)).astype(BF16)
            encoded += [acc[:, :LANES], acc[:, LANES:]]
        edge = None
        for a in range(3):
            term = jnp.dot(we[a], s_edge[:, pl.ds(3 * a * LANES, 3 * LANES)], preferred_element_type=F32)
            edge = term if edge is None else edge + term
        bias = column(0)
        pick = lambda n, there: gelu(
            jnp.where(there, edge[LANES:, n * LANES : (n + 1) * LANES], edge[:LANES, n * LANES : (n + 1) * LANES])
            + bias
        )
        above, below, beside = pick(0, turned_rows[0]), pick(1, turned_rows[1]), pick(2, turned_cols > 0)
        above = jnp.where(first_rank & (seams[0] < 0), 0.0, above).astype(BF16)
        below = jnp.where(last_rank & (seams[1] < 0), 0.0, below).astype(BF16)
        beside = jnp.where(lanes < jnp.where(seams[2] < 0, HALF, 0), 0.0, beside)
        beside = jnp.where(lanes >= jnp.where(seams[3] < 0, HALF, LANES), 0.0, beside)
        beside = close_vertices(beside, 0, HALF)
        put_rows(s_enc, [above] + encoded + [below], beside, 0, HALF)

    rounds = []
    rnd = make_round(0, [(field, 0), (field, 1)])
    late = make_round(4, [(hidden, 0), (hidden, 1)])
    rounds += [rnd, late]
    rnd.columns()
    late.columns()

    pl.semaphore_wait(barrier, len(peers))

    rnd.phase1()
    late.phase1()
    rnd.phase2()
    late.phase2()
    rnd.phase3(both, deep=True)
    late.phase3(both, deep=True)
    rnd.phase4(rnd.halo_sum())
    late.phase4(late.halo_sum())
    rnd.finish()
    stack_state(field, rnd)
    wait_for(we, wsem.at[0])
    encode()
    late.finish()
    stack_rows(hidden, late, 0, s_mem, True)
    wait_for(wh, wsem.at[2])
    for gate in range(3):
        state_conv(gate)
    wait_for(wi, wsem.at[1])
    state, memory = field, hidden

    for step in range(STEPS):
        if step > 0:
            encode()
        fresh = mems[step]
        coarse_rows = []
        for n in range(2):
            here = pl.ds(2 * n * LANES, 2 * LANES)
            gate = [conv_rows(s_enc, lambda a: wi[a, g], 2 * n) for g in range(3)]
            update = sigmoid(gate[0] + gh[0, :, here] + column(1))
            reset = sigmoid(gate[1] + gh[1, :, here] + column(2))
            candidate = jnp.tanh(gate[2] + column(3) + reset * (gh[2, :, here] + column(4)))
            pair = None
            for q in range(2):
                cut_row = slice(q * LANES, (q + 1) * LANES)
                before = flat(memory[2 * n + q]).astype(F32)
                after = (1.0 - update[:, cut_row]) * candidate[:, cut_row] + update[:, cut_row] * before
                after = after.astype(BF16)
                fresh[2 * n + q] = after.reshape(fresh.shape[1:])
                after = after.astype(F32)
                pair = after if pair is None else pair + after
            other = jnp.where(lax.rem(lanes, 2) == 0, pltpu.roll(pair, LANES - 1, 1), pltpu.roll(pair, 1, 1))
            coarse_rows.append((pair + other) * 0.25)
        coarse = coarses[step]
        for n in range(2):
            coarse[n] = coarse_rows[n].astype(BF16).reshape(coarse.shape[1:])
        sums = (
            0.5 * jnp.sum(coarse_rows[0] + coarse_rows[1], axis=1, keepdims=True),
            0.5
            * jnp.sum(
                coarse_rows[0] * coarse_rows[0] + coarse_rows[1] * coarse_rows[1], axis=1, keepdims=True
            ),
        )

        rnd = make_round(1 + 2 * step, [(fresh, 0), (coarse, 0)], extra=True)
        rounds.append(rnd)
        rnd.phase1(lambda: rnd.columns(sums))
        rnd.phase2(True)
        rnd.phase3(both, True)
        total = rnd.halo_sum()
        thin = lane_ids(cut)
        slice_here = pl.ds(pl.multiple_of(at.c * cut, cut), cut)
        gain, shift = vec[slice_here, 5:6], vec[slice_here, 6:7]

        def joint(tile):
            tile = jnp.maximum(tile, 0)
            picked = []
            for one in (tile, r["pair"][tile]):
                tx, tz, tk = split_tile(one, nz)
                lane = thin - (2 * width + 6 * (tx * 2 + tk))
                picked.append((rnd.p3[2 * tz + 1, 2].astype(F32), lane))
            result = []
            for low in (0, 3):
                masked = sum(
                    jnp.where((lane >= low) & (lane < low + 3), value, 0.0) for value, lane in picked
                )
                result.append(jnp.sum(masked, axis=1, keepdims=True))
            counted = 2 * (py // 2) * (LANES // 2)
            average = result[0] / counted
            spread = result[1] / counted - average * average
            return average, lax.rsqrt(spread + 1e-05)

        own = joint(at.t)
        stats = [joint(tile) for tile in seams + corners]

        def norm(value, average, scale):
            return gelu((value - average) * scale * gain + shift)

        extra = []
        for side in range(2):
            value = norm(total[side, 1].astype(F32), *stats[side])
            extra.append(jnp.where(seams[side] >= 0, value, 0.0))
        average = jnp.zeros((cut, LANES), F32)
        scale = jnp.zeros((cut, LANES), F32)
        valid = jnp.zeros((cut, LANES), F32)
        spans = ((2, 1, py), (3, width + 1, py), (4, 0, 1), (5, width, 1), (6, py + 1, 1), (7, width + py + 1, 1))
        for e, begin, length in spans:
            inside = (thin >= begin) & (thin < begin + length)
            average = jnp.where(inside, stats[e][0], average)
            scale = jnp.where(inside, stats[e][1], scale)
            flag = jnp.where((seams + corners)[e] >= 0, 1.0, 0.0)
            valid = jnp.where(inside, flag, valid)
        extra.append(jnp.where(valid > 0.0, norm(total[2, 1].astype(F32), average, scale), 0.0))
        colour = total[2, 1]
        for j, part in enumerate(three_parts(own[0]) + three_parts(own[1])):
            colour = jnp.where(thin == 2 * width + j, part.astype(BF16), colour)
        total[2, 1] = colour
        rnd.phase4(total, extra)
        rnd.finish()

        raw = flat(rnd.cols[:, 1]).astype(F32)
        stat_lane = lanes - 2 * width
        mean = jnp.sum(jnp.where((stat_lane >= 0) & (stat_lane < 3), raw, 0.0), axis=1, keepdims=True)
        inverse = jnp.sum(jnp.where((stat_lane >= 3) & (stat_lane < 6), raw, 0.0), axis=1, keepdims=True)
        wide = lambda value: gelu((value - mean) * inverse * column(5) + column(6))
        top, bottom = flat(rnd.up[1]).astype(F32), flat(rnd.dn[1]).astype(F32)
        active = [
            jnp.where(first_rank, flat(rnd.upx[...]).astype(F32), wide(top)),
            wide(coarse_rows[0]),
            wide(coarse_rows[1]),
            jnp.where(last_rank, flat(rnd.dnx[...]).astype(F32), wide(bottom)),
            rnd.slab_cols(2).astype(F32),
        ]
        base = [top, coarse_rows[0], coarse_rows[1], bottom, rnd.slab_cols(1).astype(F32)]
        lifted = [
            (b + jnp.dot(r["mix_w"][...], v.astype(BF16), preferred_element_type=F32)).astype(BF16)
            for b, v in zip(base, active)
        ]
        body = [lifted[0], lifted[1], lifted[1], lifted[2], lifted[2], lifted[3]]
        put_rows(s_lift, body, lifted[4], 0, width)
        stack_rows(fresh, rnd, 0, s_mem)

        if step == 0:
            wait_for(wdl, wsem.at[3])
            wait_for(wdm, wsem.at[4])
        result = r["state_out"] if step == STEPS - 1 else states[step]
        for n in range(2):
            acc = conv_rows(s_lift, lambda a: wdl[a], 2 * n) + conv_rows(s_mem, lambda a: wdm[a], 2 * n)
            acc = acc + column(7)
            for q in range(2):
                before = flat(state[2 * n + q]).astype(F32)
                after = (before + acc[:, q * LANES : (q + 1) * LANES]).astype(BF16)
                result[2 * n + q] = after.reshape(result.shape[1:])
        state, memory = result, fresh
        if step < STEPS - 1:
            rnd = make_round(2 + 2 * step, [(state, 0), (state, 1)])
            rounds.append(rnd)
            rnd.phase1(rnd.columns)
            state_conv(0)
            rnd.phase2()
            state_conv(1)
            rnd.phase3(both, deep=True)
            state_conv(2)
            rnd.phase4(rnd.halo_sum())
            rnd.finish()
            stack_state(state, rnd)

    r["memory_out"][...] = memory[...]
    for rnd in rounds:
        rnd.drain()


def on_device(
    nx, nz, ranks, py,
    field, hidden_fine, seam_tile, seam_code, corner_tile, corner_cell, pair_list, enc_weight, enc_bias,
    gru_input, gru_state, gru_bias, coarse_gain, coarse_shift, coarse_weight, dec_weight, dec_bias,
):
    cut = LANES // ranks
    vmem, anywhere = (pl.BlockSpec(memory_space=s) for s in (pltpu.VMEM, pl.ANY))
    slab = (ROWS, ranks, cut, LANES)
    scratch = [
        pltpu.VMEM((3, 2 * LANES, 3 * LANES), BF16),
        pltpu.VMEM((3, 3, LANES, 3 * LANES), BF16),
        pltpu.VMEM((3, 3, LANES, 3 * LANES), BF16),
        pltpu.VMEM((3, LANES, 3 * LANES), BF16),
        pltpu.VMEM((3, LANES, 3 * LANES), BF16),
    ]
    scratch += [pltpu.VMEM((3 * LANES, 6 * LANES), BF16) for _ in range(4)]
    scratch += [pltpu.VMEM((3 * LANES, 9 * LANES), BF16)]
    scratch += [
        pltpu.VMEM((3, LANES, ROWS * LANES), F32),
        pltpu.VMEM((2 * 3 * 2 * nx, cut, LANES), BF16),
        pltpu.SMEM((2 * nz * 12,), jnp.int32),
        pltpu.SemaphoreType.DMA((5,)),
        pltpu.VMEM((LANES, LANES), F32),
    ]
    scratch += [pltpu.VMEM(slab, BF16) for _ in range(2)]
    scratch += [pltpu.VMEM((2, ranks, cut, LANES), BF16) for _ in range(2)]
    scratch += [pltpu.VMEM(slab, BF16) for _ in range(3)] + [pltpu.VMEM((LANES, LANES), BF16)]
    scratch += [pltpu.VMEM((LANES, ROWS, LANES), BF16)] * 2
    scratch += [pltpu.SMEM((4, seam_tile.shape[0]), jnp.int32)] * 4 + [pltpu.SMEM(pair_list.shape, jnp.int32)]
    scratch += [pltpu.VMEM((LANES, LANES), BF16), pltpu.VMEM((1, LANES), F32), pltpu.VMEM((3, 2, LANES), F32)]
    scratch += [pltpu.VMEM((1, LANES), F32)] * 3 + [pltpu.SemaphoreType.DMA((13,))]
    for a, a4 in ((2, 2), (2, 3), (2, 2), (2, 3), (2, 2)):
        scratch += round_scratch(a, a4, nx, nz, ranks, cut)
    state, memory = pl.pallas_call(
        functools.partial(kernel, (nx, nz, ranks, py)),
        out_shape=[jax.ShapeDtypeStruct(slab, BF16)] * 2,
        in_specs=[anywhere] * 17,
        out_specs=[vmem] * 2,
        scratch_shapes=scratch,
        compiler_params=pltpu.CompilerParams(
            collective_id=0, has_side_effects=True, vmem_limit_bytes=107 * 2**19
        ),
    )(
        field[:, 0], hidden_fine[:, 0], seam_tile.T, seam_code.T, corner_tile.T, corner_cell.T, pair_list,
        enc_weight, gru_input, gru_state, dec_weight, coarse_weight,
        enc_bias[None], jnp.transpose(gru_bias, (1, 0, 2)), coarse_gain[None], coarse_shift[None],
        dec_bias[None],
    )
    back = lambda v: jnp.transpose(v.reshape(ROWS, LANES, LANES), (1, 0, 2))[:, None]
    return back(state), back(memory)


def solution(mesh):
    ranks = mesh.shape["chan"]
    tiles = mesh.shape["tile"]
    nz = 4 if tiles == 32 else 2
    nx = tiles // (2 * nz)
    placed = (P(None, "tile", "chan", None),) * 2
    return jax.shard_map(
        functools.partial(on_device, nx, nz, ranks, ROWS * ranks),
        mesh=mesh,
        in_specs=placed + (P(),) * 15,
        out_specs=placed,
        check_vma=False,
    )
```
